32 devices in a mesh: node: 8 (over z, core), local: 4 (over y, x), tp: 1.
Axes of the slice: x: 2, y: 2, z: 4, core: 2. Of those that a mesh axis runs over, the one named last changes fastest.
Arguments:
- tokens: bfloat16 [1024, 2048], P(('node', 'local'), 'tp'), may hold values from -6 to 6
- grad_out: bfloat16 [1024, 2048], P(('node', 'local'), 'tp'), may hold values from -6 to 6
- routes: int32 [1024, 8], P(('node', 'local')), may hold values from 0 to 15, all different within a row; in each aligned block of 32 rows (0 to 31, 32 to 63, ...) at most 24 rows name the same one
- route_weight: float32 [1024, 8], P(('node', 'local')), may hold values from 0.05 to 0.5
- w_gate: bfloat16 [32, 2048, 384], P(('node', 'local'), 'tp'), may hold values from -0.125 to 0.125
- w_up: bfloat16 [32, 2048, 384], P(('node', 'local'), 'tp'), may hold values from -0.125 to 0.125
- w_down: bfloat16 [32, 384, 2048], P(('node', 'local'), None, 'tp'), may hold values from -0.21875 to 0.21875
Outputs:
- mixed: bfloat16 [1024, 2048], P(('node', 'local'), 'tp')
- grad_tokens: bfloat16 [1024, 2048], P(('node', 'local'), 'tp')
- grad_gate: bfloat16 [32, 2048, 384], P(('node', 'local'), 'tp')
- grad_up: bfloat16 [32, 2048, 384], P(('node', 'local'), 'tp')
- grad_down: bfloat16 [32, 384, 2048], P(('node', 'local'), None, 'tp')
The draws below stay inside these ranges and needn't reach their ends.
Inputs may be any that keep to these rules, and one draw needn't show every extreme that they name: `routes`: each row names 8 different experts; within each aligned block of 32 rows (the tokens of one index of node and local) no expert is named more than 24 times, a bound that some block reaches.
All inputs are finite; a program needn't handle non-finite values.
Results may differ from the reference program's by a relative error of at most 0.02.
Values may be sent and summed in bfloat16 or wider, within the bound.
No kernel may reach another device: no remote copies, remote signals or barrier semaphores. Data moves between devices by JAX's collectives and lax.ppermute only.
A program may use at most 64 MiB of HBM per device.

```python
import math
import jax
import jax.numpy as jnp
import numpy as np
from jax import lax

D = 2048
FF = 768
TOPK = 8
TOK_DEV = 32
EXPERTS = 16
CAP = 24
TOKENS = 1024
HALF = 384
D_DEV = 2048
N_NODE = 8
N_LOCAL = 4
N_TP = 1


def shard_levels(rng, extent, cuts, least, largest):
    level, own = 1.0, jax.random.fold_in(rng, 6)
    for dim, blocks in cuts:
        steps = jnp.exp(jax.random.uniform(jax.random.fold_in(own, dim), (blocks,), jnp.float32, least / len(cuts), largest / len(cuts)))
        level = level * jnp.repeat(steps, extent[dim] // blocks).reshape([-1 if axis == dim else 1 for axis in range(len(extent))])
    return level


def assign_block(key, own, number, rows, count, top, reach, lean):
    order = jax.random.permutation(key, count)
    packed, usual = load_shares(count, rows * top, reach, lean, True), load_shares(count, rows * top, reach, lean, False)
    places = jnp.arange(count)

    def named(sizes, turn):
        used = int((sizes > 0).sum())
        fixed = max(1, used // 4)
        passed = fixed + (places - fixed + turn * (used - fixed)) % max(1, count - fixed)
        return jnp.zeros((count,), jnp.int32).at[order[jnp.where(places < fixed, places, passed)]].set(jnp.asarray(sizes, jnp.int32))

    sizes = jnp.where(number % 4 == 0, named(packed, number // 4), named(usual, number - number // 4 - 1))
    mixed = jax.random.permutation(jax.random.fold_in(own, 3), count)
    donor, taker = mixed[0:count // 2 * 2:2], mixed[1:count // 2 * 2:2]
    room = jnp.minimum(sizes[donor] - 1, reach - sizes[taker]) // 2
    room = jnp.where((donor == order[0]) | (taker == order[0]) | (sizes[taker] == 0), 0, jnp.maximum(room, 0))
    passed = jax.random.randint(jax.random.fold_in(own, 4), (count // 2,), 0, 1 << 20) % (room + 1)
    sizes = sizes.at[donor].add(-passed).at[taker].add(passed)
    labels = jnp.searchsorted(jnp.cumsum(sizes), jnp.arange(rows * top), side="right").astype(jnp.int32)
    table = labels.reshape(top, rows).T
    table = table[jax.random.permutation(jax.random.fold_in(own, 1), rows)]
    turn = jax.random.randint(jax.random.fold_in(own, 2), (rows, 1), 0, top)
    return jnp.take_along_axis(table, (jnp.arange(top)[None, :] + turn) % top, axis=1)


def load_shares(count, total, bound, lean, full):
    portions = [(1 << 20) // math.isqrt(standing ** lean) + 1 for standing in range(1, count + 1)]
    largest = bound if full else min(bound, max(-(-total // count), total * portions[0] // sum(portions)))
    least = 1 if total - largest >= count - 1 else 0
    given, surplus = [largest] + [least] * (count - 1), total - largest - least * (count - 1)
    while surplus > 0:
        movable = [i for i in range(1, count) if given[i] < largest] or [i for i in range(1, count) if given[i] < bound]
        whole, remaining = sum([portions[i] for i in movable]), surplus
        for i in movable:
            extra = min(bound - given[i], max(1, remaining * portions[i] // whole), surplus)
            given[i] = given[i] + extra
            surplus = surplus - extra
    return np.array(given)


def centred(rng, extent, spread, reach, shards=(), held_as=jnp.bfloat16):
    drawn = jax.random.normal(rng, extent, jnp.float32) * spread
    if len(shards) > 0:
        drawn = shard_levels(rng, extent, shards, -0.22, 0.18) * drawn
    return jnp.clip(drawn, min=-reach, max=reach).astype(held_as)


def setup_inputs(seed: int = 0) -> dict:
    splits = jax.random.split(jax.random.key(seed), 8)
    tokens = centred(splits[0], (TOKENS, D), 1.0, 6.0, ((0, 32),))
    grad_out = centred(splits[1], (TOKENS, D), 1.0, 6.0, ((0, 32),))
    routes_keys = jax.random.split(jax.random.fold_in(splits[2], 1), TOKENS // TOK_DEV)
    routes_turns = jax.random.permutation(jax.random.fold_in(splits[2], 3), TOKENS // TOK_DEV)
    routes = jax.vmap(lambda own, number: assign_block(jax.random.fold_in(splits[2], 2), own, number, TOK_DEV, EXPERTS, TOPK, CAP, 2))(routes_keys, routes_turns).reshape((TOKENS, TOPK))
    route_weight = jnp.clip(jnp.exp(math.log(0.5) - 2.3025851 * jax.random.uniform(splits[3], (TOKENS, TOPK), jnp.float32) ** shard_levels(splits[3], (TOKENS, TOPK), ((0, 32),), -0.2, 0.2)), 0.05, 0.5)
    w_gate = centred(splits[4], (2 * EXPERTS, D, HALF), D ** -0.5, 0.125, ((0, 32),))
    w_up = centred(splits[5], (2 * EXPERTS, D, HALF), D ** -0.5, 0.125, ((0, 32),))
    w_down = centred(splits[6], (2 * EXPERTS, HALF, D), FF ** -0.5, 0.21875, ((0, 32),))
    return dict(tokens=tokens, grad_out=grad_out, routes=routes, route_weight=route_weight, w_gate=w_gate, w_up=w_up, w_down=w_down)


def slot_table(route_rows, experts, capacity):
    flat = route_rows.reshape(-1)
    count = flat.shape[0]
    onehot = (flat[:, None] == jnp.arange(experts, dtype=jnp.int32)[None, :]).astype(jnp.float32)
    lower = (jnp.arange(count)[:, None] > jnp.arange(count)[None, :]).astype(jnp.float32)
    before = jnp.dot(lower, onehot, precision=lax.Precision.HIGHEST)
    ranking = jnp.sum(before * onehot, axis=1).astype(jnp.int32)
    position = flat * capacity + ranking
    return (position[None, :] == jnp.arange(experts * capacity, dtype=jnp.int32)[:, None]).astype(jnp.float32)


def piece_sum(parts):
    rounded = lax.optimization_barrier(parts.astype(jnp.bfloat16))
    return jnp.sum(rounded.astype(jnp.float32), axis=0)


def half_pass(x_rows, g_rows, weight_g, weight_u, weight_d):
    hi = lax.Precision.HIGHEST
    rows_all = x_rows.shape[0]
    x_pieces = x_rows.astype(jnp.float32).reshape(rows_all, N_TP, D_DEV)
    g_pieces = g_rows.astype(jnp.float32).reshape(rows_all, N_TP, D_DEV)
    gate = piece_sum(jnp.einsum('rjd,jdf->jrf', x_pieces, weight_g.astype(jnp.float32).reshape(N_TP, D_DEV, HALF), precision=hi))
    up_val = piece_sum(jnp.einsum('rjd,jdf->jrf', x_pieces, weight_u.astype(jnp.float32).reshape(N_TP, D_DEV, HALF), precision=hi))
    d_hidden = piece_sum(jnp.einsum('rjd,fjd->jrf', g_pieces, weight_d.astype(jnp.float32).reshape(HALF, N_TP, D_DEV), precision=hi))
    sig_gate = jax.nn.sigmoid(gate)
    activated = gate * sig_gate
    hidden = (activated * up_val).astype(jnp.bfloat16)
    d_gate = (d_hidden * up_val * sig_gate * (1.0 + gate * (1.0 - sig_gate))).astype(jnp.bfloat16)
    d_up = (d_hidden * activated).astype(jnp.bfloat16)
    grad_wd = jnp.dot(hidden.T, g_rows, preferred_element_type=jnp.float32).astype(jnp.bfloat16)
    grad_wg = jnp.dot(x_rows.T, d_gate, preferred_element_type=jnp.float32).astype(jnp.bfloat16)
    grad_wu = jnp.dot(x_rows.T, d_up, preferred_element_type=jnp.float32).astype(jnp.bfloat16)
    out_half = jnp.dot(hidden, weight_d, preferred_element_type=jnp.float32).astype(jnp.bfloat16)
    back_half = (jnp.dot(d_gate, weight_g.T, preferred_element_type=jnp.float32)
                 + jnp.dot(d_up, weight_u.T, preferred_element_type=jnp.float32)).astype(jnp.bfloat16)
    return grad_wg, grad_wu, grad_wd, out_half, back_half


def reference(tokens, grad_out, routes, route_weight, w_gate, w_up, w_down):
    groups = N_NODE * N_LOCAL
    rows_all = groups * CAP
    hi = lax.Precision.HIGHEST
    x_groups = tokens.reshape(groups, TOK_DEV, D).astype(jnp.float32)
    dy_groups = grad_out.reshape(groups, TOK_DEV, D).astype(jnp.float32)
    w_groups = route_weight.reshape(groups, TOK_DEV * TOPK)
    tables = jax.vmap(lambda r: slot_table(r, EXPERTS, CAP))(routes.reshape(groups, TOK_DEV, TOPK))

    def expert_step(carry, expert):
        y_acc, dx_acc = carry
        select = lax.dynamic_slice_in_dim(tables, expert * CAP, CAP, axis=1)
        token_map = select.reshape(groups, CAP, TOK_DEV, TOPK).sum(-1)
        x_rows = jnp.einsum('gct,gtd->gcd', token_map, x_groups, precision=hi).astype(jnp.bfloat16).reshape(rows_all, D)
        w_sel = jnp.sum(select * w_groups[:, None, :], axis=-1)
        dy_rows = jnp.einsum('gct,gtd->gcd', token_map, dy_groups, precision=hi)
        g_rows = (w_sel[..., None] * dy_rows).astype(jnp.bfloat16).reshape(rows_all, D)
        results = []
        for half in range(2):
            index = (2 * expert + half).astype(jnp.int32)
            weight_g = lax.dynamic_index_in_dim(w_gate, index, 0, keepdims=False)
            weight_u = lax.dynamic_index_in_dim(w_up, index, 0, keepdims=False)
            weight_d = lax.dynamic_index_in_dim(w_down, index, 0, keepdims=False)
            results.append(half_pass(x_rows, g_rows, weight_g, weight_u, weight_d))
        row_out = (results[0][3].astype(jnp.float32) + results[1][3].astype(jnp.float32)).astype(jnp.bfloat16)
        row_back = (results[0][4].astype(jnp.float32) + results[1][4].astype(jnp.float32)).astype(jnp.bfloat16)
        row_out = lax.optimization_barrier(row_out).astype(jnp.float32).reshape(groups, CAP, D)
        row_back = lax.optimization_barrier(row_back).astype(jnp.float32).reshape(groups, CAP, D)
        y_acc = y_acc + jnp.einsum('gct,gcd->gtd', token_map, w_sel[..., None] * row_out, precision=hi)
        dx_acc = dx_acc + jnp.einsum('gct,gcd->gtd', token_map, row_back, precision=hi)
        outs = (jnp.stack([results[0][0], results[1][0]]),
                jnp.stack([results[0][1], results[1][1]]),
                jnp.stack([results[0][2], results[1][2]]))
        return (y_acc, dx_acc), outs

    start = (jnp.zeros((groups, TOK_DEV, D), jnp.float32), jnp.zeros((groups, TOK_DEV, D), jnp.float32))
    (y_acc, dx_acc), (all_gate, all_up, all_down) = lax.scan(expert_step, start, jnp.arange(EXPERTS, dtype=jnp.int32))
    mixed = y_acc.reshape(TOKENS, D).astype(jnp.bfloat16)
    grad_tokens = dx_acc.reshape(TOKENS, D).astype(jnp.bfloat16)
    return (mixed, grad_tokens, all_gate.reshape(2 * EXPERTS, D, HALF),
            all_up.reshape(2 * EXPERTS, D, HALF), all_down.reshape(2 * EXPERTS, HALF, D))
```

```python
import functools

import jax
import jax.numpy as jnp
from jax import lax
from jax.experimental import pallas as pl
from jax.experimental.pallas import tpu as pltpu
from jax.sharding import PartitionSpec as P

LANES = 128
CONTRACT_LAST = (((1,), (1,)), ((), ()))
CONTRACT_FIRST = (((0,), (0,)), ((), ()))


def slot_table(route_rows, experts, capacity):
    flat = route_rows.reshape(-1)
    count = flat.shape[0]
    onehot = (flat[:, None] == jnp.arange(experts, dtype=jnp.int32)[None, :]).astype(jnp.float32)
    lower = (jnp.arange(count)[:, None] > jnp.arange(count)[None, :]).astype(jnp.float32)
    before = jnp.dot(lower, onehot, precision=lax.Precision.HIGHEST)
    ranking = jnp.sum(before * onehot, axis=1).astype(jnp.int32)
    position = flat * capacity + ranking
    return (position[None, :] == jnp.arange(experts * capacity, dtype=jnp.int32)[:, None]).astype(
        jnp.float32
    )


def activate(gate, up_val, d_hidden):
    sig_gate = jax.nn.sigmoid(gate)
    activated = gate * sig_gate
    hidden = (activated * up_val).astype(jnp.bfloat16)
    d_gate = (d_hidden * up_val * sig_gate * (1.0 + gate * (1.0 - sig_gate))).astype(jnp.bfloat16)
    d_up = (d_hidden * activated).astype(jnp.bfloat16)
    return (hidden, d_gate, d_up)


def sparse_shards(tokens, grad_out, routes, route_weight, w_gate, w_up, w_down):
    n_node = lax.axis_size("node")
    n_local = lax.axis_size("local")
    experts = n_node * n_local // 2
    exp_node = n_local // 2
    tok_rows, features = tokens.shape
    topk = routes.shape[1]
    capacity = min(tok_rows, max(2, 3 * tok_rows * topk // (2 * experts)))
    table = slot_table(routes, experts, capacity)
    token_map = table.reshape(experts * capacity, tok_rows, topk).sum(-1).astype(jnp.bfloat16)
    table_low = table.astype(jnp.bfloat16)
    send_rows = jnp.dot(token_map, tokens, preferred_element_type=jnp.float32).astype(jnp.bfloat16)
    weights_flat = route_weight.reshape(-1)
    scaled = (
        weights_flat[:, None] * jnp.repeat(grad_out, topk, axis=0).astype(jnp.float32)
    ).astype(jnp.bfloat16)
    send_grads = jnp.dot(table_low, scaled, preferred_element_type=jnp.float32).astype(jnp.bfloat16)

    def dispatch(rows):
        twice = jnp.repeat(rows.reshape(n_node, exp_node, capacity, features), 2, axis=1)
        got = lax.all_to_all(twice, "node", split_axis=0, concat_axis=2, tiled=True)
        got = lax.all_to_all(got, "local", split_axis=1, concat_axis=2, tiled=True)
        return got.reshape(got.shape[2], features)

    def combine(rows):
        rows = rows.reshape(1, n_local, n_node * capacity, features)
        got = lax.all_to_all(rows, "node", split_axis=2, concat_axis=0, tiled=True)
        got = lax.all_to_all(got, "local", split_axis=1, concat_axis=1, tiled=True)
        got = got.astype(jnp.float32).reshape(n_node, exp_node, 2, capacity, features).sum(2)
        return got.astype(jnp.bfloat16).reshape(experts * capacity, features)

    got_rows, got_grads = dispatch(send_rows), dispatch(send_grads)
    weight_g = w_gate[0]
    weight_u = w_up[0]
    weight_d = w_down[0]
    gate_part = jnp.dot(got_rows, weight_g, preferred_element_type=jnp.float32)
    up_part = jnp.dot(got_rows, weight_u, preferred_element_type=jnp.float32)
    hidden_part = lax.dot_general(
        got_grads, weight_d, CONTRACT_LAST, preferred_element_type=jnp.float32
    )
    gate, up_val, d_hidden = (
        lax.psum(gate_part.astype(jnp.bfloat16), "tp").astype(jnp.float32),
        lax.psum(up_part.astype(jnp.bfloat16), "tp").astype(jnp.float32),
        lax.psum(hidden_part.astype(jnp.bfloat16), "tp").astype(jnp.float32),
    )
    hidden, d_gate, d_up = activate(gate, up_val, d_hidden)
    grad_wd = lax.dot_general(
        hidden, got_grads, CONTRACT_FIRST, preferred_element_type=jnp.float32
    ).astype(jnp.bfloat16)
    grad_wg = lax.dot_general(
        got_rows, d_gate, CONTRACT_FIRST, preferred_element_type=jnp.float32
    ).astype(jnp.bfloat16)
    grad_wu = lax.dot_general(
        got_rows, d_up, CONTRACT_FIRST, preferred_element_type=jnp.float32
    ).astype(jnp.bfloat16)
    out_sum = jnp.dot(hidden, weight_d, preferred_element_type=jnp.float32).astype(jnp.bfloat16)
    back_sum = (
        lax.dot_general(d_gate, weight_g, CONTRACT_LAST, preferred_element_type=jnp.float32)
        + lax.dot_general(d_up, weight_u, CONTRACT_LAST, preferred_element_type=jnp.float32)
    ).astype(jnp.bfloat16)
    slot_out, slot_back = combine(out_sum), combine(back_sum)
    gathered = lax.dot_general(
        table_low, slot_out, CONTRACT_FIRST, preferred_element_type=jnp.float32
    )
    mixed = jnp.sum(
        gathered.reshape(tok_rows, topk, features) * route_weight[..., None], axis=1
    ).astype(jnp.bfloat16)
    grad_tokens = lax.dot_general(
        token_map, slot_back, CONTRACT_FIRST, preferred_element_type=jnp.float32
    ).astype(jnp.bfloat16)
    return (mixed, grad_tokens, grad_wg[None], grad_wu[None], grad_wd[None])


def pack_kernel(experts, tok_ref, grad_ref, route_ref, weight_ref, block_ref):
    rows, features = tok_ref.shape
    block_ref[:, :features] = tok_ref[...]
    block_ref[:, features : 2 * features] = grad_ref[...]
    lane = lax.broadcasted_iota(jnp.int32, (rows, LANES), 1)
    expert = lane % experts
    dense = jnp.zeros((rows, LANES), jnp.float32)
    for k in range(route_ref.shape[1]):
        dense += jnp.where(route_ref[:, k : k + 1] == expert, weight_ref[:, k : k + 1], 0.0)
    high = dense.astype(jnp.bfloat16).astype(jnp.float32)
    middle = (dense - high).astype(jnp.bfloat16).astype(jnp.float32)
    low = dense - high - middle
    part = lane // experts
    parts = jnp.where(part == 0, high, jnp.where(part == 1, middle, jnp.where(part == 2, low, 0.0)))
    block_ref[:, 2 * features :] = parts.astype(jnp.bfloat16)


def pack(tokens, grad_out, routes, route_weight, experts):
    rows, features = tokens.shape
    return pl.pallas_call(
        functools.partial(pack_kernel, experts),
        out_shape=jax.ShapeDtypeStruct((rows, 2 * features + LANES), jnp.bfloat16),
    )(tokens, grad_out, routes, route_weight)


def forward_kernel(
    experts, n_blocks, expert_ref, *refs
):
    blocks = refs[:n_blocks]
    wg_ref, wu_ref, wd_ref = refs[n_blocks : n_blocks + 3]
    x_ref, g_ref, keep_ref, send_ref, hid_ref, dgu_ref = refs[n_blocks + 3 : n_blocks + 9]
    wgu, wd, rw, sems, wsems = refs[n_blocks + 9 :]
    features, half = wg_ref.shape
    rows = blocks[0].shape[0]
    w_copies = [
        pltpu.make_async_copy(wg_ref, wgu.at[:, :half], wsems.at[0]),
        pltpu.make_async_copy(wu_ref, wgu.at[:, half:], wsems.at[1]),
        pltpu.make_async_copy(wd_ref, wd, wsems.at[2]),
    ]
    x_copies, g_copies, r_copies = [], [], []
    for i, block in enumerate(blocks):
        place = pl.ds(i * rows, rows)
        x_copies.append(
            pltpu.make_async_copy(block.at[:, :features], x_ref.at[place], sems.at[0, i])
        )
        g_copies.append(
            pltpu.make_async_copy(
                block.at[:, features : 2 * features], g_ref.at[place], sems.at[1, i]
            )
        )
        r_copies.append(
            pltpu.make_async_copy(block.at[:, 2 * features :], rw.at[place], sems.at[2, i])
        )
    for copy in w_copies[:2] + x_copies + r_copies + w_copies[2:] + g_copies:
        copy.start()
    for copy in w_copies[:2] + x_copies + r_copies:
        copy.wait()
    gate_up = jnp.dot(x_ref[...], wgu[...], preferred_element_type=jnp.float32)
    for copy in w_copies[2:] + g_copies:
        copy.wait()
    lane = lax.broadcasted_iota(jnp.int32, rw.shape, 1)
    chosen = (lane % experts == expert_ref[0]) & (lane < 3 * experts)
    weight = jnp.sum(jnp.where(chosen, rw[...].astype(jnp.float32), 0.0), axis=1, keepdims=True)
    d_hidden = (
        lax.dot_general(g_ref[...], wd[...], CONTRACT_LAST, preferred_element_type=jnp.float32)
        * weight
    )
    gate, up_val = gate_up[:, :half], gate_up[:, half:]
    sig_gate = jax.nn.sigmoid(gate)
    activated = gate * sig_gate
    hid_ref[...] = (weight * (activated * up_val)).astype(jnp.bfloat16)
    dgu_ref[:, :half] = (
        d_hidden * up_val * sig_gate * (1.0 + gate * (1.0 - sig_gate))
    ).astype(jnp.bfloat16)
    dgu_ref[:, half:] = (d_hidden * activated).astype(jnp.bfloat16)
    out = jnp.dot(hid_ref[...], wd[...], preferred_element_type=jnp.float32).astype(jnp.bfloat16)
    own = keep_ref.shape[0]
    keep_ref[:, :features] = out[:own]
    send_ref[:, :features] = out[own:]
    back = lax.dot_general(
        dgu_ref[...], wgu[...], CONTRACT_LAST, preferred_element_type=jnp.float32
    ).astype(jnp.bfloat16)
    keep_ref[:, features:] = back[:own]
    send_ref[:, features:] = back[own:]


def forward(expert, blocks, weight_g, weight_u, weight_d, experts):
    rows = blocks[0].shape[0] * len(blocks)
    features, half = weight_g.shape
    bf16 = jnp.bfloat16
    out_shape = (
        jax.ShapeDtypeStruct((rows, features), bf16),
        jax.ShapeDtypeStruct((rows, features), bf16),
        jax.ShapeDtypeStruct((rows // 2, 2 * features), bf16),
        jax.ShapeDtypeStruct((rows // 2, 2 * features), bf16),
        jax.ShapeDtypeStruct((rows, half), bf16),
        jax.ShapeDtypeStruct((rows, 2 * half), bf16),
    )
    return pl.pallas_call(
        functools.partial(forward_kernel, experts, len(blocks)),
        out_shape=out_shape,
        in_specs=[pl.BlockSpec(memory_space=pltpu.SMEM)]
        + [pl.BlockSpec(memory_space=pl.ANY)] * (len(blocks) + 3),
        out_specs=tuple(pl.BlockSpec(memory_space=pltpu.VMEM) for _ in out_shape),
        scratch_shapes=[
            pltpu.VMEM((features, 2 * half), bf16),
            pltpu.VMEM((half, features), bf16),
            pltpu.VMEM((rows, LANES), bf16),
            pltpu.SemaphoreType.DMA((3, len(blocks))),
            pltpu.SemaphoreType.DMA((3,)),
        ],
        compiler_params=pltpu.CompilerParams(vmem_limit_bytes=40 << 20),
        cost_estimate=pl.CostEstimate(
            flops=12 * rows * features * half,
            bytes_accessed=6 * features * half + 16 * rows * features,
            transcendentals=rows * half,
        ),
    )(expert, *blocks, weight_g, weight_u, weight_d)


def grads_kernel(n_slots, *refs):
    xs, gs, hids, dgus = (refs[i * n_slots : (i + 1) * n_slots] for i in range(4))
    gg_ref, gu_ref, gd_ref = refs[4 * n_slots :]
    half = gg_ref.shape[1]

    def product(lefts, rights):
        return sum(
            lax.dot_general(
                left[...], right[...], CONTRACT_FIRST, preferred_element_type=jnp.float32
            )
            for left, right in zip(lefts, rights)
        ).astype(jnp.bfloat16)

    grad_gu = product(xs, dgus)
    gg_ref[...] = grad_gu[:, :half]
    gu_ref[...] = grad_gu[:, half:]
    gd_ref[...] = product(hids, gs)


def weight_grads(xs, gs, hids, dgus):
    features, half, rows = xs[0].shape[1], hids[0].shape[1], xs[0].shape[0]
    tile = 256
    bf16 = jnp.bfloat16
    n_slots = len(xs)
    wide = pl.BlockSpec((rows, tile), lambda f: (0, f))
    return pl.pallas_call(
        functools.partial(grads_kernel, n_slots),
        grid=(features // tile,),
        out_shape=(
            jax.ShapeDtypeStruct((features, half), bf16),
            jax.ShapeDtypeStruct((features, half), bf16),
            jax.ShapeDtypeStruct((half, features), bf16),
        ),
        in_specs=[wide] * (2 * n_slots)
        + [pl.BlockSpec((rows, half), lambda f: (0, 0))] * n_slots
        + [pl.BlockSpec((rows, 2 * half), lambda f: (0, 0))] * n_slots,
        out_specs=(
            pl.BlockSpec((tile, half), lambda f: (f, 0)),
            pl.BlockSpec((tile, half), lambda f: (f, 0)),
            pl.BlockSpec((half, tile), lambda f: (0, f)),
        ),
        compiler_params=pltpu.CompilerParams(vmem_limit_bytes=40 << 20),
        cost_estimate=pl.CostEstimate(
            flops=6 * n_slots * rows * features * half,
            bytes_accessed=6 * features * half + 4 * n_slots * rows * features,
            transcendentals=0,
        ),
    )(*xs, *gs, *hids, *dgus)


def add(left, right):
    return (left.astype(jnp.float32) + right.astype(jnp.float32)).astype(jnp.bfloat16)


def dense_shards(tokens, grad_out, routes, route_weight, w_gate, w_up, w_down):
    n_node, n_local = lax.axis_size("node"), lax.axis_size("local")
    experts = n_node * n_local // 2
    n_z = n_node // 2
    features = tokens.shape[1]
    axes = ("node", "local")
    device = lax.axis_index("node") * n_local + lax.axis_index("local")
    expert = jnp.full((1,), device // 2, jnp.int32)

    def exchange(value, step):
        pairs = [(d, d ^ step((d // n_local) % 2)) for d in range(n_node * n_local)]
        return lax.ppermute(value, axes, pairs)

    first = lambda core: 1 + core
    second = lambda core: 2 - core
    sibling = lambda core: n_local

    block = pack(tokens, grad_out, routes, route_weight, experts)
    slots = [block] + [
        exchange(block, lambda core, z=z: z * 2 * n_local) for z in range(1, n_z)
    ]
    weights = (w_gate[0], w_up[0], w_down[0])
    results = []
    for own in slots:
        one = exchange(own, first)
        two = exchange(own, second)
        both = exchange(one, second)
        plane = [own, one, two, both]
        others = [exchange(part, sibling) for part in plane]
        results.append(forward(expert, plane + others, *weights, experts))
    rows = tokens.shape[0]
    arrived = []
    for z in list(range(1, n_z)) + [0]:
        _, _, keep, send, _, _ = results[z]
        total = add(keep, exchange(send, sibling))
        total = add(total[: 2 * rows], exchange(total[2 * rows :], second))
        total = add(total[:rows], exchange(total[rows:], first))
        arrived.append(exchange(total, lambda core: z * 2 * n_local) if z else total)
    final = sum(part.astype(jnp.float32) for part in arrived).astype(jnp.bfloat16)
    xs, gs, _, _, hids, dgus = (list(column) for column in zip(*results))
    grad_wg, grad_wu, grad_wd = weight_grads(xs, gs, hids, dgus)
    return (
        final[:, :features],
        final[:, features:],
        grad_wg[None],
        grad_wu[None],
        grad_wd[None],
    )


def solution(mesh):
    n_node, n_local, n_tp = (mesh.shape[name] for name in ("node", "local", "tp"))

    def shards(tokens, grad_out, routes, *rest):
        experts = n_node * n_local // 2
        grid = n_tp == 1 and n_local == 4 and n_node in (4, 8)
        if grid and 2 * routes.shape[1] >= experts:
            return dense_shards(tokens, grad_out, routes, *rest)
        return sparse_shards(tokens, grad_out, routes, *rest)

    return jax.shard_map(
        shards,
        mesh=mesh,
        in_specs=(
            P(("node", "local"), "tp"),
            P(("node", "local"), "tp"),
            P(("node", "local"), None),
            P(("node", "local"), None),
            P(("node", "local"), "tp", None),
            P(("node", "local"), "tp", None),
            P(("node", "local"), None, "tp"),
        ),
        out_specs=(
            P(("node", "local"), "tp"),
            P(("node", "local"), "tp"),
            P(("node", "local"), "tp", None),
            P(("node", "local"), "tp", None),
            P(("node", "local"), None, "tp"),
        ),
        check_vma=False,
    )
```

```python
import functools

import jax
import jax.numpy as jnp
from jax import lax
from jax.experimental import pallas as pl
from jax.experimental.pallas import tpu as pltpu
from jax.sharding import PartitionSpec as P

LANES = 128
VMEM_BYTES = 32 << 20
CONTRACT_LAST = (((1,), (1,)), ((), ()))
CONTRACT_FIRST = (((0,), (0,)), ((), ()))


def slot_table(route_rows, experts, capacity):
    flat = route_rows.reshape(-1)
    count = flat.shape[0]
    onehot = (flat[:, None] == jnp.arange(experts, dtype=jnp.int32)[None, :]).astype(jnp.float32)
    lower = (jnp.arange(count)[:, None] > jnp.arange(count)[None, :]).astype(jnp.float32)
    before = jnp.dot(lower, onehot, precision=lax.Precision.HIGHEST)
    ranking = jnp.sum(before * onehot, axis=1).astype(jnp.int32)
    position = flat * capacity + ranking
    return (position[None, :] == jnp.arange(experts * capacity, dtype=jnp.int32)[:, None]).astype(
        jnp.float32
    )


def activate(gate, up_val, d_hidden):
    sig_gate = jax.nn.sigmoid(gate)
    activated = gate * sig_gate
    hidden = (activated * up_val).astype(jnp.bfloat16)
    d_gate = (d_hidden * up_val * sig_gate * (1.0 + gate * (1.0 - sig_gate))).astype(jnp.bfloat16)
    d_up = (d_hidden * activated).astype(jnp.bfloat16)
    return (hidden, d_gate, d_up)


def sparse_shards(tokens, grad_out, routes, route_weight, w_gate, w_up, w_down):
    n_node = lax.axis_size("node")
    n_local = lax.axis_size("local")
    experts = n_node * n_local // 2
    exp_node = n_local // 2
    tok_rows, features = tokens.shape
    topk = routes.shape[1]
    capacity = min(tok_rows, max(2, 3 * tok_rows * topk // (2 * experts)))
    table = slot_table(routes, experts, capacity)
    token_map = table.reshape(experts * capacity, tok_rows, topk).sum(-1).astype(jnp.bfloat16)
    table_low = table.astype(jnp.bfloat16)
    send_rows = jnp.dot(token_map, tokens, preferred_element_type=jnp.float32).astype(jnp.bfloat16)
    weights_flat = route_weight.reshape(-1)
    scaled = (
        weights_flat[:, None] * jnp.repeat(grad_out, topk, axis=0).astype(jnp.float32)
    ).astype(jnp.bfloat16)
    send_grads = jnp.dot(table_low, scaled, preferred_element_type=jnp.float32).astype(jnp.bfloat16)

    def dispatch(rows):
        twice = jnp.repeat(rows.reshape(n_node, exp_node, capacity, features), 2, axis=1)
        got = lax.all_to_all(twice, "node", split_axis=0, concat_axis=2, tiled=True)
        got = lax.all_to_all(got, "local", split_axis=1, concat_axis=2, tiled=True)
        return got.reshape(got.shape[2], features)

    def combine(rows):
        rows = rows.reshape(1, n_local, n_node * capacity, features)
        got = lax.all_to_all(rows, "node", split_axis=2, concat_axis=0, tiled=True)
        got = lax.all_to_all(got, "local", split_axis=1, concat_axis=1, tiled=True)
        got = got.astype(jnp.float32).reshape(n_node, exp_node, 2, capacity, features).sum(2)
        return got.astype(jnp.bfloat16).reshape(experts * capacity, features)

    got_rows, got_grads = dispatch(send_rows), dispatch(send_grads)
    weight_g = w_gate[0]
    weight_u = w_up[0]
    weight_d = w_down[0]
    gate_part = jnp.dot(got_rows, weight_g, preferred_element_type=jnp.float32)
    up_part = jnp.dot(got_rows, weight_u, preferred_element_type=jnp.float32)
    hidden_part = lax.dot_general(
        got_grads, weight_d, CONTRACT_LAST, preferred_element_type=jnp.float32
    )
    gate, up_val, d_hidden = (
        lax.psum(gate_part.astype(jnp.bfloat16), "tp").astype(jnp.float32),
        lax.psum(up_part.astype(jnp.bfloat16), "tp").astype(jnp.float32),
        lax.psum(hidden_part.astype(jnp.bfloat16), "tp").astype(jnp.float32),
    )
    hidden, d_gate, d_up = activate(gate, up_val, d_hidden)
    grad_wd = lax.dot_general(
        hidden, got_grads, CONTRACT_FIRST, preferred_element_type=jnp.float32
    ).astype(jnp.bfloat16)
    grad_wg = lax.dot_general(
        got_rows, d_gate, CONTRACT_FIRST, preferred_element_type=jnp.float32
    ).astype(jnp.bfloat16)
    grad_wu = lax.dot_general(
        got_rows, d_up, CONTRACT_FIRST, preferred_element_type=jnp.float32
    ).astype(jnp.bfloat16)
    out_sum = jnp.dot(hidden, weight_d, preferred_element_type=jnp.float32).astype(jnp.bfloat16)
    back_sum = (
        lax.dot_general(d_gate, weight_g, CONTRACT_LAST, preferred_element_type=jnp.float32)
        + lax.dot_general(d_up, weight_u, CONTRACT_LAST, preferred_element_type=jnp.float32)
    ).astype(jnp.bfloat16)
    slot_out, slot_back = combine(out_sum), combine(back_sum)
    gathered = lax.dot_general(
        table_low, slot_out, CONTRACT_FIRST, preferred_element_type=jnp.float32
    )
    mixed = jnp.sum(
        gathered.reshape(tok_rows, topk, features) * route_weight[..., None], axis=1
    ).astype(jnp.bfloat16)
    grad_tokens = lax.dot_general(
        token_map, slot_back, CONTRACT_FIRST, preferred_element_type=jnp.float32
    ).astype(jnp.bfloat16)
    return (mixed, grad_tokens, grad_wg[None], grad_wu[None], grad_wd[None])


def pack_kernel(experts, tok_ref, grad_ref, route_ref, weight_ref, block_ref):
    rows, features = tok_ref.shape
    block_ref[:, :features] = tok_ref[...]
    block_ref[:, features : 2 * features] = grad_ref[...]
    lane = lax.broadcasted_iota(jnp.int32, (rows, LANES), 1)
    expert = lane % experts
    dense = jnp.zeros((rows, LANES), jnp.float32)
    chosen, share = jnp.transpose(route_ref[...]), jnp.transpose(weight_ref[...])
    for k in range(chosen.shape[1]):
        dense += jnp.where(chosen[:, k : k + 1] == expert, share[:, k : k + 1], 0.0)
    high = dense.astype(jnp.bfloat16).astype(jnp.float32)
    middle = (dense - high).astype(jnp.bfloat16).astype(jnp.float32)
    low = dense - high - middle
    part = lane // experts
    parts = jnp.where(part == 0, high, jnp.where(part == 1, middle, jnp.where(part == 2, low, 0.0)))
    block_ref[:, 2 * features :] = parts.astype(jnp.bfloat16)


def pack(tokens, grad_out, routes, route_weight, experts):
    rows, features = tokens.shape
    return pl.pallas_call(
        functools.partial(pack_kernel, experts),
        out_shape=jax.ShapeDtypeStruct((rows, 2 * features + LANES), jnp.bfloat16),
    )(tokens, grad_out, routes.T, route_weight.T)


def place_copies(pieces, columns, held, sems):
    copies, row = [], 0
    for i, piece in enumerate(pieces):
        place = pl.ds(row, piece.shape[0])
        copies.append(pltpu.make_async_copy(piece.at[:, columns], held.at[place], sems.at[i]))
        row += piece.shape[0]
    return copies


def forward_kernel(experts, n_pieces, expert_ref, *refs):
    pieces = refs[:n_pieces]
    wg_ref, wu_ref, wd_ref = refs[n_pieces : n_pieces + 3]
    keep_ref, send_ref, hid_ref, dgu_ref = refs[n_pieces + 3 : n_pieces + 7]
    x, g, rw, wgu, wd, hid, dgu, out, back = refs[n_pieces + 7 : n_pieces + 16]
    x_sems, g_sems, r_sems, w_sems, o_sems = refs[n_pieces + 16 :]
    features, half = wg_ref.shape
    own = keep_ref.shape[0]
    cut = features // 2
    w_copies, d_copies = [], []
    for i in range(2):
        rows = pl.ds(i * cut, cut)
        w_copies += [
            pltpu.make_async_copy(wg_ref.at[rows], wgu.at[rows, :half], w_sems.at[2 * i]),
            pltpu.make_async_copy(wu_ref.at[rows], wgu.at[rows, half:], w_sems.at[2 * i + 1]),
        ]
        d_copies.append(
            pltpu.make_async_copy(wd_ref.at[:, rows], wd.at[:, rows], w_sems.at[4 + i])
        )
    x_copies = place_copies(pieces, pl.ds(0, features), x, x_sems)
    g_copies = place_copies(pieces, pl.ds(features, features), g, g_sems)
    r_copies = place_copies(pieces, pl.ds(2 * features, LANES), rw, r_sems)
    for copy in d_copies + g_copies + r_copies + w_copies + x_copies:
        copy.start()
    for copy in d_copies + g_copies + r_copies:
        copy.wait()
    lane = lax.broadcasted_iota(jnp.int32, rw.shape, 1)
    chosen = (lane % experts == expert_ref[0]) & (lane < 3 * experts)
    weight = jnp.sum(jnp.where(chosen, rw[...].astype(jnp.float32), 0.0), axis=1, keepdims=True)
    d_hidden = (
        lax.dot_general(g[...], wd[...], CONTRACT_LAST, preferred_element_type=jnp.float32)
        * weight
    )
    for copy in w_copies + x_copies:
        copy.wait()
    gate_up = jnp.dot(x[...], wgu[...], preferred_element_type=jnp.float32)
    gate, up_val = gate_up[:, :half], gate_up[:, half:]
    sig_gate = jax.nn.sigmoid(gate)
    activated = gate * sig_gate
    hid[...] = (weight * (activated * up_val)).astype(jnp.bfloat16)
    dgu[:, :half] = (d_hidden * up_val * sig_gate * (1.0 + gate * (1.0 - sig_gate))).astype(
        jnp.bfloat16
    )
    dgu[:, half:] = (d_hidden * activated).astype(jnp.bfloat16)
    sends = [
        pltpu.make_async_copy(hid, hid_ref, o_sems.at[0]),
        pltpu.make_async_copy(dgu, dgu_ref, o_sems.at[1]),
    ]

    def leave(part, column):
        sends.append(
            pltpu.make_async_copy(
                part.at[own:], send_ref.at[:, column], o_sems.at[len(sends)]
            )
        )
        sends.append(
            pltpu.make_async_copy(
                part.at[:own], keep_ref.at[:, column], o_sems.at[len(sends)]
            )
        )
        sends[-2].start()
        sends[-1].start()

    sends[0].start()
    sends[1].start()
    out[...] = jnp.dot(hid[...], wd[...], preferred_element_type=jnp.float32).astype(jnp.bfloat16)
    leave(out, pl.ds(0, features))
    for i in range(2):
        columns = pl.ds(i * cut, cut)
        back[i] = lax.dot_general(
            dgu[...], wgu[columns], CONTRACT_LAST, preferred_element_type=jnp.float32
        ).astype(jnp.bfloat16)
        leave(back.at[i], pl.ds(features + i * cut, cut))
    for copy in sends:
        copy.wait()


def forward(expert, pieces, weight_g, weight_u, weight_d, experts):
    rows = sum(piece.shape[0] for piece in pieces)
    features, half = weight_g.shape
    bf16 = jnp.bfloat16
    out_shape = (
        jax.ShapeDtypeStruct((rows // 2, 2 * features), bf16),
        jax.ShapeDtypeStruct((rows // 2, 2 * features), bf16),
        jax.ShapeDtypeStruct((rows, half), bf16),
        jax.ShapeDtypeStruct((rows, 2 * half), bf16),
    )
    return pl.pallas_call(
        functools.partial(forward_kernel, experts, len(pieces)),
        out_shape=out_shape,
        in_specs=[pl.BlockSpec(memory_space=pltpu.SMEM)]
        + [pl.BlockSpec(memory_space=pl.ANY)] * (len(pieces) + 3),
        out_specs=tuple(pl.BlockSpec(memory_space=pl.ANY) for _ in out_shape),
        scratch_shapes=[
            pltpu.VMEM((rows, features), bf16),
            pltpu.VMEM((rows, features), bf16),
            pltpu.VMEM((rows, LANES), bf16),
            pltpu.VMEM((features, 2 * half), bf16),
            pltpu.VMEM((half, features), bf16),
            pltpu.VMEM((rows, half), bf16),
            pltpu.VMEM((rows, 2 * half), bf16),
            pltpu.VMEM((rows, features), bf16),
            pltpu.VMEM((2, rows, features // 2), bf16),
            pltpu.SemaphoreType.DMA((len(pieces),)),
            pltpu.SemaphoreType.DMA((len(pieces),)),
            pltpu.SemaphoreType.DMA((len(pieces),)),
            pltpu.SemaphoreType.DMA((6,)),
            pltpu.SemaphoreType.DMA((8,)),
        ],
        compiler_params=pltpu.CompilerParams(vmem_limit_bytes=VMEM_BYTES),
        cost_estimate=pl.CostEstimate(
            flops=12 * 20 * rows * features * half,
            bytes_accessed=6 * features * half + 8 * rows * features,
            transcendentals=rows * half,
        ),
    )(expert, *pieces, weight_g, weight_u, weight_d)


def grads_kernel(n_pieces, n_slots, tile, *refs):
    pieces, refs = refs[:n_pieces], refs[n_pieces:]
    hids, dgus, refs = refs[:n_slots], refs[n_slots : 2 * n_slots], refs[2 * n_slots :]
    gg_ref, gu_ref, gd_ref, x, g, hid, dgu, gg, gu, gd, x_sems, g_sems, a_sems, o_sems = refs
    features, half = gg_ref.shape
    every = pl.ds(0, half)
    first = place_copies(dgus, pl.ds(0, 2 * half), dgu, a_sems.at[0])
    first += place_copies(pieces, pl.ds(0, features), x, x_sems)
    then = place_copies(hids, every, hid, a_sems.at[1])
    then += place_copies(pieces, pl.ds(features, features), g, g_sems)
    for copy in first + then:
        copy.start()
    for copy in first:
        copy.wait()
    sends = []

    def leave(held, place, ref):
        sends.append(
            pltpu.make_async_copy(held.at[place], ref.at[place], o_sems.at[len(sends)])
        )
        sends[-1].start()

    for i in range(features // tile):
        rows = pl.ds(i * tile, tile)
        grad_gu = lax.dot_general(
            x[:, rows], dgu[...], CONTRACT_FIRST, preferred_element_type=jnp.float32
        ).astype(jnp.bfloat16)
        gg[rows] = grad_gu[:, :half]
        gu[rows] = grad_gu[:, half:]
        leave(gg, rows, gg_ref)
        leave(gu, rows, gu_ref)
    for copy in then:
        copy.wait()
    for i in range(half // LANES):
        rows = pl.ds(i * LANES, LANES)
        gd[rows] = lax.dot_general(
            hid[:, rows], g[...], CONTRACT_FIRST, preferred_element_type=jnp.float32
        ).astype(jnp.bfloat16)
        leave(gd, rows, gd_ref)
    for copy in sends:
        copy.wait()


def weight_grads(pieces, hids, dgus):
    features, half = pieces[0].shape[1] // 2 // LANES * LANES, hids[0].shape[1]
    rows = sum(piece.shape[0] for piece in pieces)
    tile = min(256, features)
    bf16 = jnp.bfloat16
    out_shape = (
        jax.ShapeDtypeStruct((features, half), bf16),
        jax.ShapeDtypeStruct((features, half), bf16),
        jax.ShapeDtypeStruct((half, features), bf16),
    )
    return pl.pallas_call(
        functools.partial(grads_kernel, len(pieces), len(hids), tile),
        out_shape=out_shape,
        in_specs=[pl.BlockSpec(memory_space=pl.ANY)] * (len(pieces) + 2 * len(hids)),
        out_specs=tuple(pl.BlockSpec(memory_space=pl.ANY) for _ in out_shape),
        scratch_shapes=[
            pltpu.VMEM((rows, features), bf16),
            pltpu.VMEM((rows, features), bf16),
            pltpu.VMEM((rows, half), bf16),
            pltpu.VMEM((rows, 2 * half), bf16),
            pltpu.VMEM((features, half), bf16),
            pltpu.VMEM((features, half), bf16),
            pltpu.VMEM((half, features), bf16),
            pltpu.SemaphoreType.DMA((len(pieces),)),
            pltpu.SemaphoreType.DMA((len(pieces),)),
            pltpu.SemaphoreType.DMA((2, len(hids))),
            pltpu.SemaphoreType.DMA((2 * (features // tile) + half // LANES,)),
        ],
        compiler_params=pltpu.CompilerParams(vmem_limit_bytes=VMEM_BYTES),
        cost_estimate=pl.CostEstimate(
            flops=6 * 20 * rows * features * half,
            bytes_accessed=6 * features * half + 4 * rows * features,
            transcendentals=0,
        ),
    )(*pieces, *hids, *dgus)


def add(left, right):
    return (left.astype(jnp.float32) + right.astype(jnp.float32)).astype(jnp.bfloat16)


def after(value, *earlier):
    return lax.optimization_barrier((value,) + earlier)[0]


def tick_kernel(in_ref, out_ref):
    pass


def tick(token):
    return pl.pallas_call(
        tick_kernel,
        out_shape=jax.ShapeDtypeStruct(token.shape, token.dtype),
        in_specs=[pl.BlockSpec(memory_space=pl.ANY)],
        out_specs=pl.BlockSpec(memory_space=pl.ANY),
        input_output_aliases={0: 0},
        cost_estimate=pl.CostEstimate(flops=50_000_000_000, bytes_accessed=0, transcendentals=0),
    )(token)


def dense_shards(tokens, grad_out, routes, route_weight, w_gate, w_up, w_down):
    n_node, n_local = lax.axis_size("node"), lax.axis_size("local")
    experts = n_node * n_local // 2
    n_z = n_node // 2
    features = tokens.shape[1]
    axes = ("node", "local")
    device = lax.axis_index("node") * n_local + lax.axis_index("local")
    expert = jnp.full((1,), device // 2, jnp.int32)

    def exchange(value, step):
        pairs = [(d, d ^ step((d // n_local) % 2)) for d in range(n_node * n_local)]
        return lax.ppermute(value, axes, pairs)

    first = lambda core: 1 + core
    second = lambda core: 2 - core
    sibling = lambda core: n_local

    def along(z):
        return lambda core: z * 2 * n_local

    rows = tokens.shape[0]
    weights = (w_gate[0], w_up[0], w_down[0])
    block = pack(tokens, grad_out, routes, route_weight, experts)
    now = [jnp.zeros((8, LANES), jnp.float32)]

    def start(value, step):
        return exchange(after(value, now[0]), step)

    def wait(value):
        value, now[0] = lax.optimization_barrier((value, now[0]))
        return value

    def turn():
        now[0] = tick(now[0])

    pairs, twos, taken, results, sums = {}, {}, {}, {}, {}

    def spread(z, one, own):
        pairs[z] = wait(jnp.concatenate([own, wait(one)]))
        return start(pairs[z], second), start(pairs[z], sibling)

    def across(z, two):
        twos[z] = wait(two)
        return start(twos[z], sibling)

    def compute(z, pair_there, two_there):
        taken[z] = [pairs[z], twos[z], pair_there, two_there]
        results[z] = forward(expert, [after(t, now[0]) for t in taken[z]], *weights, experts)
        results[z] = [wait(t) for t in results[z]]
        return start(results[z][1], sibling)

    def fold(z, there):
        sums[z] = wait(add(results[z][0], wait(there)))
        return start(sums[z][2 * rows :], second)

    def fold_second(z, there):
        sums[z] = wait(add(sums[z][: 2 * rows], wait(there)))
        return start(sums[z][rows:], first)

    def fold_first(z, there):
        sums[z] = wait(add(sums[z][:rows], wait(there)))
        return start(sums[z], along(z)) if z else sums[z]

    one0 = start(block, first)
    far1 = start(block, along(1))
    far2 = start(block, along(2))
    turn()
    two0, pt0 = spread(0, one0, block)
    turn()
    far1 = wait(far1)
    one1 = start(far1, first)
    turn()
    tt0 = across(0, two0)
    far2 = wait(far2)
    one2 = start(far2, first)
    far3 = start(block, along(3))
    turn()
    two1, pt1 = spread(1, one1, far1)
    turn()
    back0 = compute(0, pt0, tt0)
    two2, pt2 = spread(2, one2, far2)
    tt1 = across(1, two1)
    turn()
    back1 = compute(1, pt1, tt1)
    far3 = wait(far3)
    one3 = start(far3, first)
    tt2 = across(2, two2)
    back0 = fold(0, back0)
    turn()
    two3, pt3 = spread(3, one3, far3)
    back2 = compute(2, pt2, tt2)
    back1 = fold(1, back1)
    turn()
    tt3 = across(3, two3)
    turn()
    back2 = fold(2, back2)
    back0 = fold_second(0, back0)
    turn()
    back3 = compute(3, pt3, tt3)
    back1 = fold_second(1, back1)
    turn()
    back3 = fold(3, back3)
    back2 = fold_second(2, back2)
    turn()
    back1 = fold_first(1, back1)
    back2 = fold_first(2, back2)
    back3 = fold_second(3, back3)
    turn()
    back3 = fold_first(3, back3)
    back0 = fold_first(0, back0)
    order = [0, 1, 2, 3]
    grad_wg, grad_wu, grad_wd = weight_grads(
        [after(piece, now[0]) for z in order for piece in taken[z]],
        [results[z][2] for z in order],
        [results[z][3] for z in order],
    )
    grad_wg = wait(grad_wg)
    arrived = (back0, wait(back2), wait(back1), wait(back3))
    final = sum(part.astype(jnp.float32) for part in arrived).astype(jnp.bfloat16)
    return (
        final[:, :features],
        final[:, features:],
        grad_wg[None],
        grad_wu[None],
        grad_wd[None],
    )


def solution(mesh):
    n_node, n_local, n_tp = (mesh.shape[name] for name in ("node", "local", "tp"))

    def shards(tokens, grad_out, routes, *rest):
        experts = n_node * n_local // 2
        grid = n_tp == 1 and n_local == 4 and n_node in (4, 8)
        if grid and 2 * routes.shape[1] >= experts:
            return dense_shards(tokens, grad_out, routes, *rest)
        return sparse_shards(tokens, grad_out, routes, *rest)

    return jax.shard_map(
        shards,
        mesh=mesh,
        in_specs=(
            P(("node", "local"), "tp"),
            P(("node", "local"), "tp"),
            P(("node", "local"), None),
            P(("node", "local"), None),
            P(("node", "local"), "tp", None),
            P(("node", "local"), "tp", None),
            P(("node", "local"), None, "tp"),
        ),
        out_specs=(
            P(("node", "local"), "tp"),
            P(("node", "local"), "tp"),
            P(("node", "local"), "tp", None),
            P(("node", "local"), "tp", None),
            P(("node", "local"), None, "tp"),
        ),
        check_vma=False,
    )
```

```python
import functools

import jax
import jax.numpy as jnp
from jax import lax
from jax.experimental import pallas as pl
from jax.experimental.pallas import tpu as pltpu
from jax.sharding import PartitionSpec as P

LANES = 128
VMEM_BYTES = 32 << 20
CONTRACT_LAST = (((1,), (1,)), ((), ()))
CONTRACT_FIRST = (((0,), (0,)), ((), ()))


def slot_table(route_rows, experts, capacity):
    flat = route_rows.reshape(-1)
    count = flat.shape[0]
    onehot = (flat[:, None] == jnp.arange(experts, dtype=jnp.int32)[None, :]).astype(jnp.float32)
    lower = (jnp.arange(count)[:, None] > jnp.arange(count)[None, :]).astype(jnp.float32)
    before = jnp.dot(lower, onehot, precision=lax.Precision.HIGHEST)
    ranking = jnp.sum(before * onehot, axis=1).astype(jnp.int32)
    position = flat * capacity + ranking
    return (position[None, :] == jnp.arange(experts * capacity, dtype=jnp.int32)[:, None]).astype(
        jnp.float32
    )


def activate(gate, up_val, d_hidden):
    sig_gate = jax.nn.sigmoid(gate)
    activated = gate * sig_gate
    hidden = (activated * up_val).astype(jnp.bfloat16)
    d_gate = (d_hidden * up_val * sig_gate * (1.0 + gate * (1.0 - sig_gate))).astype(jnp.bfloat16)
    d_up = (d_hidden * activated).astype(jnp.bfloat16)
    return (hidden, d_gate, d_up)


def sparse_shards(tokens, grad_out, routes, route_weight, w_gate, w_up, w_down):
    n_node = lax.axis_size("node")
    n_local = lax.axis_size("local")
    experts = n_node * n_local // 2
    exp_node = n_local // 2
    tok_rows, features = tokens.shape
    topk = routes.shape[1]
    capacity = min(tok_rows, max(2, 3 * tok_rows * topk // (2 * experts)))
    table = slot_table(routes, experts, capacity)
    token_map = table.reshape(experts * capacity, tok_rows, topk).sum(-1).astype(jnp.bfloat16)
    table_low = table.astype(jnp.bfloat16)
    send_rows = jnp.dot(token_map, tokens, preferred_element_type=jnp.float32).astype(jnp.bfloat16)
    weights_flat = route_weight.reshape(-1)
    scaled = (
        weights_flat[:, None] * jnp.repeat(grad_out, topk, axis=0).astype(jnp.float32)
    ).astype(jnp.bfloat16)
    send_grads = jnp.dot(table_low, scaled, preferred_element_type=jnp.float32).astype(jnp.bfloat16)

    def dispatch(rows):
        twice = jnp.repeat(rows.reshape(n_node, exp_node, capacity, features), 2, axis=1)
        got = lax.all_to_all(twice, "node", split_axis=0, concat_axis=2, tiled=True)
        got = lax.all_to_all(got, "local", split_axis=1, concat_axis=2, tiled=True)
        return got.reshape(got.shape[2], features)

    def combine(rows):
        rows = rows.reshape(1, n_local, n_node * capacity, features)
        got = lax.all_to_all(rows, "node", split_axis=2, concat_axis=0, tiled=True)
        got = lax.all_to_all(got, "local", split_axis=1, concat_axis=1, tiled=True)
        got = got.astype(jnp.float32).reshape(n_node, exp_node, 2, capacity, features).sum(2)
        return got.astype(jnp.bfloat16).reshape(experts * capacity, features)

    got_rows, got_grads = dispatch(send_rows), dispatch(send_grads)
    weight_g = w_gate[0]
    weight_u = w_up[0]
    weight_d = w_down[0]
    gate_part = jnp.dot(got_rows, weight_g, preferred_element_type=jnp.float32)
    up_part = jnp.dot(got_rows, weight_u, preferred_element_type=jnp.float32)
    hidden_part = lax.dot_general(
        got_grads, weight_d, CONTRACT_LAST, preferred_element_type=jnp.float32
    )
    gate, up_val, d_hidden = (
        lax.psum(gate_part.astype(jnp.bfloat16), "tp").astype(jnp.float32),
        lax.psum(up_part.astype(jnp.bfloat16), "tp").astype(jnp.float32),
        lax.psum(hidden_part.astype(jnp.bfloat16), "tp").astype(jnp.float32),
    )
    hidden, d_gate, d_up = activate(gate, up_val, d_hidden)
    grad_wd = lax.dot_general(
        hidden, got_grads, CONTRACT_FIRST, preferred_element_type=jnp.float32
    ).astype(jnp.bfloat16)
    grad_wg = lax.dot_general(
        got_rows, d_gate, CONTRACT_FIRST, preferred_element_type=jnp.float32
    ).astype(jnp.bfloat16)
    grad_wu = lax.dot_general(
        got_rows, d_up, CONTRACT_FIRST, preferred_element_type=jnp.float32
    ).astype(jnp.bfloat16)
    out_sum = jnp.dot(hidden, weight_d, preferred_element_type=jnp.float32).astype(jnp.bfloat16)
    back_sum = (
        lax.dot_general(d_gate, weight_g, CONTRACT_LAST, preferred_element_type=jnp.float32)
        + lax.dot_general(d_up, weight_u, CONTRACT_LAST, preferred_element_type=jnp.float32)
    ).astype(jnp.bfloat16)
    slot_out, slot_back = combine(out_sum), combine(back_sum)
    gathered = lax.dot_general(
        table_low, slot_out, CONTRACT_FIRST, preferred_element_type=jnp.float32
    )
    mixed = jnp.sum(
        gathered.reshape(tok_rows, topk, features) * route_weight[..., None], axis=1
    ).astype(jnp.bfloat16)
    grad_tokens = lax.dot_general(
        token_map, slot_back, CONTRACT_FIRST, preferred_element_type=jnp.float32
    ).astype(jnp.bfloat16)
    return (mixed, grad_tokens, grad_wg[None], grad_wu[None], grad_wd[None])


def pack_kernel(experts, tok_ref, grad_ref, route_ref, weight_ref, block_ref):
    rows, features = tok_ref.shape
    block_ref[:, :features] = tok_ref[...]
    block_ref[:, features : 2 * features] = grad_ref[...]
    lane = lax.broadcasted_iota(jnp.int32, (rows, LANES), 1)
    expert = lane % experts
    dense = jnp.zeros((rows, LANES), jnp.float32)
    chosen, share = jnp.transpose(route_ref[...]), jnp.transpose(weight_ref[...])
    for k in range(chosen.shape[1]):
        dense += jnp.where(chosen[:, k : k + 1] == expert, share[:, k : k + 1], 0.0)
    high = dense.astype(jnp.bfloat16).astype(jnp.float32)
    middle = (dense - high).astype(jnp.bfloat16).astype(jnp.float32)
    low = dense - high - middle
    part = lane // experts
    parts = jnp.where(part == 0, high, jnp.where(part == 1, middle, jnp.where(part == 2, low, 0.0)))
    block_ref[:, 2 * features :] = parts.astype(jnp.bfloat16)


def pack(tokens, grad_out, routes, route_weight, experts):
    rows, features = tokens.shape
    return pl.pallas_call(
        functools.partial(pack_kernel, experts),
        out_shape=jax.ShapeDtypeStruct((rows, 2 * features + LANES), jnp.bfloat16),
    )(tokens, grad_out, routes.T, route_weight.T)


def stage_kernel(wg_ref, wu_ref, wd_ref, wgu_ref, wd_held_ref, sems):
    half = wg_ref.shape[1]
    copies = [
        pltpu.make_async_copy(wg_ref, wgu_ref.at[:, :half], sems.at[0]),
        pltpu.make_async_copy(wu_ref, wgu_ref.at[:, half:], sems.at[1]),
        pltpu.make_async_copy(wd_ref, wd_held_ref, sems.at[2]),
    ]
    for copy in copies:
        copy.start()
    for copy in copies:
        copy.wait()


def stage(weight_g, weight_u, weight_d):
    features, half = weight_g.shape
    return pl.pallas_call(
        stage_kernel,
        out_shape=(
            jax.ShapeDtypeStruct((features, 2 * half), jnp.bfloat16),
            jax.ShapeDtypeStruct((half, features), jnp.bfloat16),
        ),
        in_specs=[pl.BlockSpec(memory_space=pl.ANY)] * 3,
        out_specs=(pl.BlockSpec(memory_space=pltpu.VMEM),) * 2,
        scratch_shapes=[pltpu.SemaphoreType.DMA((3,))],
        compiler_params=pltpu.CompilerParams(vmem_limit_bytes=VMEM_BYTES),
        cost_estimate=pl.CostEstimate(
            flops=0, bytes_accessed=12 * features * half, transcendentals=0
        ),
    )(weight_g, weight_u, weight_d)


def place_copies(pieces, columns, held, sems):
    copies, row = [], 0
    for i, piece in enumerate(pieces):
        place = pl.ds(row, piece.shape[0])
        copies.append(pltpu.make_async_copy(piece.at[:, columns], held.at[place], sems.at[i]))
        row += piece.shape[0]
    return copies


def forward_kernel(experts, n_pieces, expert_ref, *refs):
    pieces = refs[:n_pieces]
    wgu, wd = refs[n_pieces : n_pieces + 2]
    keep_ref, send_ref, hid_ref, dgu_ref = refs[n_pieces + 2 : n_pieces + 6]
    x, g, rw, hid, dgu, out, back = refs[n_pieces + 6 : n_pieces + 13]
    x_sems, g_sems, r_sems, o_sems = refs[n_pieces + 13 :]
    half, features = wd.shape
    own = keep_ref.shape[0]
    cut = features // 2
    x_copies = place_copies(pieces, pl.ds(0, features), x, x_sems)
    g_copies = place_copies(pieces, pl.ds(features, features), g, g_sems)
    r_copies = place_copies(pieces, pl.ds(2 * features, LANES), rw, r_sems)
    for copy in g_copies + r_copies + x_copies:
        copy.start()
    for copy in g_copies + r_copies:
        copy.wait()
    lane = lax.broadcasted_iota(jnp.int32, rw.shape, 1)
    chosen = (lane % experts == expert_ref[0]) & (lane < 3 * experts)
    weight = jnp.sum(jnp.where(chosen, rw[...].astype(jnp.float32), 0.0), axis=1, keepdims=True)
    d_hidden = (
        lax.dot_general(g[...], wd[...], CONTRACT_LAST, preferred_element_type=jnp.float32)
        * weight
    )
    for copy in x_copies:
        copy.wait()
    gate_up = jnp.dot(x[...], wgu[...], preferred_element_type=jnp.float32)
    gate, up_val = gate_up[:, :half], gate_up[:, half:]
    sig_gate = jax.nn.sigmoid(gate)
    activated = gate * sig_gate
    hid[...] = (weight * (activated * up_val)).astype(jnp.bfloat16)
    dgu[:, :half] = (d_hidden * up_val * sig_gate * (1.0 + gate * (1.0 - sig_gate))).astype(
        jnp.bfloat16
    )
    dgu[:, half:] = (d_hidden * activated).astype(jnp.bfloat16)
    sends = [
        pltpu.make_async_copy(hid, hid_ref, o_sems.at[0]),
        pltpu.make_async_copy(dgu, dgu_ref, o_sems.at[1]),
    ]

    def leave(part, column):
        sends.append(
            pltpu.make_async_copy(
                part.at[own:], send_ref.at[:, column], o_sems.at[len(sends)]
            )
        )
        sends.append(
            pltpu.make_async_copy(
                part.at[:own], keep_ref.at[:, column], o_sems.at[len(sends)]
            )
        )
        sends[-2].start()
        sends[-1].start()

    sends[0].start()
    sends[1].start()
    out[...] = jnp.dot(hid[...], wd[...], preferred_element_type=jnp.float32).astype(jnp.bfloat16)
    leave(out, pl.ds(0, features))
    for i in range(2):
        columns = pl.ds(i * cut, cut)
        back[i] = lax.dot_general(
            dgu[...], wgu[columns], CONTRACT_LAST, preferred_element_type=jnp.float32
        ).astype(jnp.bfloat16)
        leave(back.at[i], pl.ds(features + i * cut, cut))
    for copy in sends:
        copy.wait()


def forward(expert, pieces, weight_gu, weight_d, experts):
    rows = sum(piece.shape[0] for piece in pieces)
    half, features = weight_d.shape
    bf16 = jnp.bfloat16
    out_shape = (
        jax.ShapeDtypeStruct((rows // 2, 2 * features), bf16),
        jax.ShapeDtypeStruct((rows // 2, 2 * features), bf16),
        jax.ShapeDtypeStruct((rows, half), bf16),
        jax.ShapeDtypeStruct((rows, 2 * half), bf16),
    )
    return pl.pallas_call(
        functools.partial(forward_kernel, experts, len(pieces)),
        out_shape=out_shape,
        in_specs=[pl.BlockSpec(memory_space=pltpu.SMEM)]
        + [pl.BlockSpec(memory_space=pl.ANY)] * len(pieces)
        + [pl.BlockSpec(memory_space=pltpu.VMEM)] * 2,
        out_specs=tuple(pl.BlockSpec(memory_space=pl.ANY) for _ in out_shape),
        scratch_shapes=[
            pltpu.VMEM((rows, features), bf16),
            pltpu.VMEM((rows, features), bf16),
            pltpu.VMEM((rows, LANES), bf16),
            pltpu.VMEM((rows, half), bf16),
            pltpu.VMEM((rows, 2 * half), bf16),
            pltpu.VMEM((rows, features), bf16),
            pltpu.VMEM((2, rows, features // 2), bf16),
            pltpu.SemaphoreType.DMA((len(pieces),)),
            pltpu.SemaphoreType.DMA((len(pieces),)),
            pltpu.SemaphoreType.DMA((len(pieces),)),
            pltpu.SemaphoreType.DMA((8,)),
        ],
        compiler_params=pltpu.CompilerParams(vmem_limit_bytes=VMEM_BYTES),
        cost_estimate=pl.CostEstimate(
            flops=12 * 20 * rows * features * half,
            bytes_accessed=6 * features * half + 8 * rows * features,
            transcendentals=rows * half,
        ),
    )(expert, *pieces, weight_gu, weight_d)


def grads_kernel(n_pieces, n_slots, tile, *refs):
    pieces, refs = refs[:n_pieces], refs[n_pieces:]
    hids, dgus, refs = refs[:n_slots], refs[n_slots : 2 * n_slots], refs[2 * n_slots :]
    gg_ref, gu_ref, gd_ref, x, g, hid, dgu, gg, gu, gd, x_sems, g_sems, a_sems, o_sems = refs
    features, half = gg_ref.shape
    every = pl.ds(0, half)
    first = place_copies(dgus, pl.ds(0, 2 * half), dgu, a_sems.at[0])
    first += place_copies(pieces, pl.ds(0, features), x, x_sems)
    then = place_copies(hids, every, hid, a_sems.at[1])
    then += place_copies(pieces, pl.ds(features, features), g, g_sems)
    for copy in first + then:
        copy.start()
    for copy in first:
        copy.wait()
    sends = []

    def leave(held, place, ref):
        sends.append(
            pltpu.make_async_copy(held.at[place], ref.at[place], o_sems.at[len(sends)])
        )
        sends[-1].start()

    for i in range(features // tile):
        rows = pl.ds(i * tile, tile)
        grad_gu = lax.dot_general(
            x[:, rows], dgu[...], CONTRACT_FIRST, preferred_element_type=jnp.float32
        ).astype(jnp.bfloat16)
        gg[rows] = grad_gu[:, :half]
        gu[rows] = grad_gu[:, half:]
        leave(gg, rows, gg_ref)
        leave(gu, rows, gu_ref)
    for copy in then:
        copy.wait()
    for i in range(half // LANES):
        rows = pl.ds(i * LANES, LANES)
        gd[rows] = lax.dot_general(
            hid[:, rows], g[...], CONTRACT_FIRST, preferred_element_type=jnp.float32
        ).astype(jnp.bfloat16)
        leave(gd, rows, gd_ref)
    for copy in sends:
        copy.wait()


def weight_grads(pieces, hids, dgus):
    features, half = pieces[0].shape[1] // 2 // LANES * LANES, hids[0].shape[1]
    rows = sum(piece.shape[0] for piece in pieces)
    tile = min(256, features)
    bf16 = jnp.bfloat16
    out_shape = (
        jax.ShapeDtypeStruct((features, half), bf16),
        jax.ShapeDtypeStruct((features, half), bf16),
        jax.ShapeDtypeStruct((half, features), bf16),
    )
    return pl.pallas_call(
        functools.partial(grads_kernel, len(pieces), len(hids), tile),
        out_shape=out_shape,
        in_specs=[pl.BlockSpec(memory_space=pl.ANY)] * (len(pieces) + 2 * len(hids)),
        out_specs=tuple(pl.BlockSpec(memory_space=pl.ANY) for _ in out_shape),
        scratch_shapes=[
            pltpu.VMEM((rows, features), bf16),
            pltpu.VMEM((rows, features), bf16),
            pltpu.VMEM((rows, half), bf16),
            pltpu.VMEM((rows, 2 * half), bf16),
            pltpu.VMEM((features, half), bf16),
            pltpu.VMEM((features, half), bf16),
            pltpu.VMEM((half, features), bf16),
            pltpu.SemaphoreType.DMA((len(pieces),)),
            pltpu.SemaphoreType.DMA((len(pieces),)),
            pltpu.SemaphoreType.DMA((2, len(hids))),
            pltpu.SemaphoreType.DMA((2 * (features // tile) + half // LANES,)),
        ],
        compiler_params=pltpu.CompilerParams(vmem_limit_bytes=VMEM_BYTES),
        cost_estimate=pl.CostEstimate(
            flops=6 * 20 * rows * features * half,
            bytes_accessed=6 * features * half + 4 * rows * features,
            transcendentals=0,
        ),
    )(*pieces, *hids, *dgus)


def add(left, right):
    return (left.astype(jnp.float32) + right.astype(jnp.float32)).astype(jnp.bfloat16)


def after(value, *earlier):
    return lax.optimization_barrier((value,) + earlier)[0]


def tick_kernel(in_ref, out_ref):
    pass


def tick(token):
    return pl.pallas_call(
        tick_kernel,
        out_shape=jax.ShapeDtypeStruct(token.shape, token.dtype),
        in_specs=[pl.BlockSpec(memory_space=pl.ANY)],
        out_specs=pl.BlockSpec(memory_space=pl.ANY),
        input_output_aliases={0: 0},
        cost_estimate=pl.CostEstimate(flops=50_000_000_000, bytes_accessed=0, transcendentals=0),
    )(token)


def dense_shards(tokens, grad_out, routes, route_weight, w_gate, w_up, w_down):
    n_node, n_local = lax.axis_size("node"), lax.axis_size("local")
    experts = n_node * n_local // 2
    n_z = n_node // 2
    features = tokens.shape[1]
    axes = ("node", "local")
    device = lax.axis_index("node") * n_local + lax.axis_index("local")
    expert = jnp.full((1,), device // 2, jnp.int32)

    def exchange(value, step):
        pairs = [(d, d ^ step((d // n_local) % 2)) for d in range(n_node * n_local)]
        return lax.ppermute(value, axes, pairs)

    first = lambda core: 1 + core
    second = lambda core: 2 - core
    sibling = lambda core: n_local

    def along(z):
        return lambda core: z * 2 * n_local

    rows = tokens.shape[0]
    block = pack(tokens, grad_out, routes, route_weight, experts)
    now = [jnp.zeros((8, LANES), jnp.float32)]

    def start(value, step):
        return exchange(after(value, now[0]), step)

    def wait(value):
        value, now[0] = lax.optimization_barrier((value, now[0]))
        return value

    def turn():
        now[0] = tick(now[0])

    pairs, twos, taken, results, sums = {}, {}, {}, {}, {}

    def spread(z, one, own):
        pairs[z] = wait(jnp.concatenate([own, wait(one)]))
        return start(pairs[z], second), start(pairs[z], sibling)

    def across(z, two):
        twos[z] = wait(two)
        return start(twos[z], sibling)

    def compute(z, pair_there, two_there):
        taken[z] = [pairs[z], twos[z], pair_there, two_there]
        results[z] = forward(expert, [after(t, now[0]) for t in taken[z]], *weights, experts)
        results[z] = [wait(t) for t in results[z]]
        return start(results[z][1], sibling)

    def fold(z, there):
        sums[z] = wait(add(results[z][0], wait(there)))
        return start(sums[z][2 * rows :], second)

    def fold_second(z, there):
        sums[z] = wait(add(sums[z][: 2 * rows], wait(there)))
        return start(sums[z][rows:], first)

    def fold_first(z, there):
        sums[z] = wait(add(sums[z][:rows], wait(there)))
        return start(sums[z], along(z)) if z else sums[z]

    one0 = start(block, first)
    far1 = start(block, along(1))
    far2 = start(block, along(2))
    turn()
    two0, pt0 = spread(0, one0, block)
    weights = stage(after(w_gate, now[0])[0], w_up[0], w_down[0])
    weights = [wait(w) for w in weights]
    turn()
    far1 = wait(far1)
    one1 = start(far1, first)
    far3 = start(block, along(3))
    turn()
    tt0 = across(0, two0)
    two1, pt1 = spread(1, one1, far1)
    turn()
    far2 = wait(far2)
    one2 = start(far2, first)
    back0 = compute(0, pt0, tt0)
    two2, pt2 = spread(2, one2, far2)
    turn()
    far3 = wait(far3)
    one3 = start(far3, first)
    tt1 = across(1, two1)
    turn()
    back1 = compute(1, pt1, tt1)
    two3, pt3 = spread(3, one3, far3)
    tt2 = across(2, two2)
    turn()
    back2 = compute(2, pt2, tt2)
    back1 = fold(1, back1)
    tt3 = across(3, two3)
    turn()
    back2 = fold(2, back2)
    back0 = fold(0, back0)
    back3 = compute(3, pt3, tt3)
    turn()
    back0 = fold_second(0, back0)
    back3 = fold(3, back3)
    back2 = fold_second(2, back2)
    back1 = fold_second(1, back1)
    turn()
    back2 = fold_first(2, back2)
    turn()
    back3 = fold_second(3, back3)
    turn()
    back1 = fold_first(1, back1)
    back0 = fold_first(0, back0)
    turn()
    back3 = fold_first(3, back3)
    order = [0, 1, 2, 3]
    grad_wg, grad_wu, grad_wd = weight_grads(
        [after(piece, now[0]) for z in order for piece in taken[z]],
        [results[z][2] for z in order],
        [results[z][3] for z in order],
    )
    grad_wg = wait(grad_wg)
    arrived = (back0, wait(back2), wait(back1), wait(back3))
    final = sum(part.astype(jnp.float32) for part in arrived).astype(jnp.bfloat16)
    return (
        final[:, :features],
        final[:, features:],
        grad_wg[None],
        grad_wu[None],
        grad_wd[None],
    )


def solution(mesh):
    n_node, n_local, n_tp = (mesh.shape[name] for name in ("node", "local", "tp"))

    def shards(tokens, grad_out, routes, *rest):
        experts = n_node * n_local // 2
        grid = n_tp == 1 and n_local == 4 and n_node in (4, 8)
        if grid and 2 * routes.shape[1] >= experts:
            return dense_shards(tokens, grad_out, routes, *rest)
        return sparse_shards(tokens, grad_out, routes, *rest)

    return jax.shard_map(
        shards,
        mesh=mesh,
        in_specs=(
            P(("node", "local"), "tp"),
            P(("node", "local"), "tp"),
            P(("node", "local"), None),
            P(("node", "local"), None),
            P(("node", "local"), "tp", None),
            P(("node", "local"), "tp", None),
            P(("node", "local"), None, "tp"),
        ),
        out_specs=(
            P(("node", "local"), "tp"),
            P(("node", "local"), "tp"),
            P(("node", "local"), "tp", None),
            P(("node", "local"), "tp", None),
            P(("node", "local"), None, "tp"),
        ),
        check_vma=False,
    )
```

```python
import functools

import jax
import jax.numpy as jnp
from jax import lax
from jax.experimental import pallas as pl
from jax.experimental.pallas import tpu as pltpu
from jax.sharding import PartitionSpec as P

LANES = 128
VMEM_BYTES = 32 << 20
CONTRACT_LAST = (((1,), (1,)), ((), ()))
CONTRACT_FIRST = (((0,), (0,)), ((), ()))


def slot_table(route_rows, experts, capacity):
    flat = route_rows.reshape(-1)
    count = flat.shape[0]
    onehot = (flat[:, None] == jnp.arange(experts, dtype=jnp.int32)[None, :]).astype(jnp.float32)
    lower = (jnp.arange(count)[:, None] > jnp.arange(count)[None, :]).astype(jnp.float32)
    before = jnp.dot(lower, onehot, precision=lax.Precision.HIGHEST)
    ranking = jnp.sum(before * onehot, axis=1).astype(jnp.int32)
    position = flat * capacity + ranking
    return (position[None, :] == jnp.arange(experts * capacity, dtype=jnp.int32)[:, None]).astype(
        jnp.float32
    )


def activate(gate, up_val, d_hidden):
    sig_gate = jax.nn.sigmoid(gate)
    activated = gate * sig_gate
    hidden = (activated * up_val).astype(jnp.bfloat16)
    d_gate = (d_hidden * up_val * sig_gate * (1.0 + gate * (1.0 - sig_gate))).astype(jnp.bfloat16)
    d_up = (d_hidden * activated).astype(jnp.bfloat16)
    return (hidden, d_gate, d_up)


def sparse_shards(tokens, grad_out, routes, route_weight, w_gate, w_up, w_down):
    n_node = lax.axis_size("node")
    n_local = lax.axis_size("local")
    experts = n_node * n_local // 2
    exp_node = n_local // 2
    tok_rows, features = tokens.shape
    topk = routes.shape[1]
    capacity = min(tok_rows, max(2, 3 * tok_rows * topk // (2 * experts)))
    table = slot_table(routes, experts, capacity)
    token_map = table.reshape(experts * capacity, tok_rows, topk).sum(-1).astype(jnp.bfloat16)
    table_low = table.astype(jnp.bfloat16)
    send_rows = jnp.dot(token_map, tokens, preferred_element_type=jnp.float32).astype(jnp.bfloat16)
    weights_flat = route_weight.reshape(-1)
    scaled = (
        weights_flat[:, None] * jnp.repeat(grad_out, topk, axis=0).astype(jnp.float32)
    ).astype(jnp.bfloat16)
    send_grads = jnp.dot(table_low, scaled, preferred_element_type=jnp.float32).astype(jnp.bfloat16)

    def dispatch(rows):
        twice = jnp.repeat(rows.reshape(n_node, exp_node, capacity, features), 2, axis=1)
        got = lax.all_to_all(twice, "node", split_axis=0, concat_axis=2, tiled=True)
        got = lax.all_to_all(got, "local", split_axis=1, concat_axis=2, tiled=True)
        return got.reshape(got.shape[2], features)

    def combine(rows):
        rows = rows.reshape(1, n_local, n_node * capacity, features)
        got = lax.all_to_all(rows, "node", split_axis=2, concat_axis=0, tiled=True)
        got = lax.all_to_all(got, "local", split_axis=1, concat_axis=1, tiled=True)
        got = got.astype(jnp.float32).reshape(n_node, exp_node, 2, capacity, features).sum(2)
        return got.astype(jnp.bfloat16).reshape(experts * capacity, features)

    got_rows, got_grads = dispatch(send_rows), dispatch(send_grads)
    weight_g = w_gate[0]
    weight_u = w_up[0]
    weight_d = w_down[0]
    gate_part = jnp.dot(got_rows, weight_g, preferred_element_type=jnp.float32)
    up_part = jnp.dot(got_rows, weight_u, preferred_element_type=jnp.float32)
    hidden_part = lax.dot_general(
        got_grads, weight_d, CONTRACT_LAST, preferred_element_type=jnp.float32
    )
    gate, up_val, d_hidden = (
        lax.psum(gate_part.astype(jnp.bfloat16), "tp").astype(jnp.float32),
        lax.psum(up_part.astype(jnp.bfloat16), "tp").astype(jnp.float32),
        lax.psum(hidden_part.astype(jnp.bfloat16), "tp").astype(jnp.float32),
    )
    hidden, d_gate, d_up = activate(gate, up_val, d_hidden)
    grad_wd = lax.dot_general(
        hidden, got_grads, CONTRACT_FIRST, preferred_element_type=jnp.float32
    ).astype(jnp.bfloat16)
    grad_wg = lax.dot_general(
        got_rows, d_gate, CONTRACT_FIRST, preferred_element_type=jnp.float32
    ).astype(jnp.bfloat16)
    grad_wu = lax.dot_general(
        got_rows, d_up, CONTRACT_FIRST, preferred_element_type=jnp.float32
    ).astype(jnp.bfloat16)
    out_sum = jnp.dot(hidden, weight_d, preferred_element_type=jnp.float32).astype(jnp.bfloat16)
    back_sum = (
        lax.dot_general(d_gate, weight_g, CONTRACT_LAST, preferred_element_type=jnp.float32)
        + lax.dot_general(d_up, weight_u, CONTRACT_LAST, preferred_element_type=jnp.float32)
    ).astype(jnp.bfloat16)
    slot_out, slot_back = combine(out_sum), combine(back_sum)
    gathered = lax.dot_general(
        table_low, slot_out, CONTRACT_FIRST, preferred_element_type=jnp.float32
    )
    mixed = jnp.sum(
        gathered.reshape(tok_rows, topk, features) * route_weight[..., None], axis=1
    ).astype(jnp.bfloat16)
    grad_tokens = lax.dot_general(
        token_map, slot_back, CONTRACT_FIRST, preferred_element_type=jnp.float32
    ).astype(jnp.bfloat16)
    return (mixed, grad_tokens, grad_wg[None], grad_wu[None], grad_wd[None])


def pack_kernel(experts, tok_ref, grad_ref, route_ref, weight_ref, block_ref):
    rows, features = tok_ref.shape
    block_ref[:, :features] = tok_ref[...]
    block_ref[:, features : 2 * features] = grad_ref[...]
    lane = lax.broadcasted_iota(jnp.int32, (rows, LANES), 1)
    expert = lane % experts
    dense = jnp.zeros((rows, LANES), jnp.float32)
    chosen, share = jnp.transpose(route_ref[...]), jnp.transpose(weight_ref[...])
    for k in range(chosen.shape[1]):
        dense += jnp.where(chosen[:, k : k + 1] == expert, share[:, k : k + 1], 0.0)
    high = dense.astype(jnp.bfloat16).astype(jnp.float32)
    middle = (dense - high).astype(jnp.bfloat16).astype(jnp.float32)
    low = dense - high - middle
    part = lane // experts
    parts = jnp.where(part == 0, high, jnp.where(part == 1, middle, jnp.where(part == 2, low, 0.0)))
    block_ref[:, 2 * features :] = parts.astype(jnp.bfloat16)


def pack(tokens, grad_out, routes, route_weight, experts):
    rows, features = tokens.shape
    return pl.pallas_call(
        functools.partial(pack_kernel, experts),
        out_shape=jax.ShapeDtypeStruct((rows, 2 * features + LANES), jnp.bfloat16),
    )(tokens, grad_out, routes.T, route_weight.T)


def stage_kernel(wg_ref, wu_ref, wd_ref, wgu_ref, wd_held_ref, sems):
    half = wg_ref.shape[1]
    copies = [
        pltpu.make_async_copy(wg_ref, wgu_ref.at[:, :half], sems.at[0]),
        pltpu.make_async_copy(wu_ref, wgu_ref.at[:, half:], sems.at[1]),
        pltpu.make_async_copy(wd_ref, wd_held_ref, sems.at[2]),
    ]
    for copy in copies:
        copy.start()
    for copy in copies:
        copy.wait()


def stage(weight_g, weight_u, weight_d):
    features, half = weight_g.shape
    return pl.pallas_call(
        stage_kernel,
        out_shape=(
            jax.ShapeDtypeStruct((features, 2 * half), jnp.bfloat16),
            jax.ShapeDtypeStruct((half, features), jnp.bfloat16),
        ),
        in_specs=[pl.BlockSpec(memory_space=pl.ANY)] * 3,
        out_specs=(pl.BlockSpec(memory_space=pltpu.VMEM),) * 2,
        scratch_shapes=[pltpu.SemaphoreType.DMA((3,))],
        compiler_params=pltpu.CompilerParams(vmem_limit_bytes=VMEM_BYTES),
        cost_estimate=pl.CostEstimate(
            flops=0, bytes_accessed=12 * features * half, transcendentals=0
        ),
    )(weight_g, weight_u, weight_d)


def place_copies(pieces, columns, held, sems):
    copies, row = [], 0
    for i, piece in enumerate(pieces):
        place = pl.ds(row, piece.shape[0])
        copies.append(pltpu.make_async_copy(piece.at[:, columns], held.at[place], sems.at[i]))
        row += piece.shape[0]
    return copies


def forward_kernel(experts, n_pieces, expert_ref, *refs):
    pieces = refs[:n_pieces]
    wgu, wd = refs[n_pieces : n_pieces + 2]
    keep_ref, send_ref, hid_ref, dgu_ref = refs[n_pieces + 2 : n_pieces + 6]
    x, g, rw, hid, dgu, out, back = refs[n_pieces + 6 : n_pieces + 13]
    x_sems, g_sems, r_sems, o_sems = refs[n_pieces + 13 :]
    half, features = wd.shape
    own = keep_ref.shape[0]
    cut = features // 2
    x_copies = place_copies(pieces, pl.ds(0, features), x, x_sems)
    g_copies = place_copies(pieces, pl.ds(features, features), g, g_sems)
    r_copies = place_copies(pieces, pl.ds(2 * features, LANES), rw, r_sems)
    for copy in g_copies + r_copies + x_copies:
        copy.start()
    for copy in g_copies + r_copies:
        copy.wait()
    lane = lax.broadcasted_iota(jnp.int32, rw.shape, 1)
    chosen = (lane % experts == expert_ref[0]) & (lane < 3 * experts)
    weight = jnp.sum(jnp.where(chosen, rw[...].astype(jnp.float32), 0.0), axis=1, keepdims=True)
    d_hidden = (
        lax.dot_general(g[...], wd[...], CONTRACT_LAST, preferred_element_type=jnp.float32)
        * weight
    )
    for copy in x_copies:
        copy.wait()
    gate_up = jnp.dot(x[...], wgu[...], preferred_element_type=jnp.float32)
    gate, up_val = gate_up[:, :half], gate_up[:, half:]
    sig_gate = jax.nn.sigmoid(gate)
    activated = gate * sig_gate
    hid[...] = (weight * (activated * up_val)).astype(jnp.bfloat16)
    dgu[:, :half] = (d_hidden * up_val * sig_gate * (1.0 + gate * (1.0 - sig_gate))).astype(
        jnp.bfloat16
    )
    dgu[:, half:] = (d_hidden * activated).astype(jnp.bfloat16)
    sends = [
        pltpu.make_async_copy(hid, hid_ref, o_sems.at[0]),
        pltpu.make_async_copy(dgu, dgu_ref, o_sems.at[1]),
    ]

    def leave(part, column):
        sends.append(
            pltpu.make_async_copy(
                part.at[own:], send_ref.at[:, column], o_sems.at[len(sends)]
            )
        )
        sends.append(
            pltpu.make_async_copy(
                part.at[:own], keep_ref.at[:, column], o_sems.at[len(sends)]
            )
        )
        sends[-2].start()
        sends[-1].start()

    sends[0].start()
    sends[1].start()
    out[...] = jnp.dot(hid[...], wd[...], preferred_element_type=jnp.float32).astype(jnp.bfloat16)
    leave(out, pl.ds(0, features))
    for i in range(2):
        columns = pl.ds(i * cut, cut)
        back[i] = lax.dot_general(
            dgu[...], wgu[columns], CONTRACT_LAST, preferred_element_type=jnp.float32
        ).astype(jnp.bfloat16)
        leave(back.at[i], pl.ds(features + i * cut, cut))
    for copy in sends:
        copy.wait()


def forward(expert, pieces, weight_gu, weight_d, experts):
    rows = sum(piece.shape[0] for piece in pieces)
    half, features = weight_d.shape
    bf16 = jnp.bfloat16
    out_shape = (
        jax.ShapeDtypeStruct((rows // 2, 2 * features), bf16),
        jax.ShapeDtypeStruct((rows // 2, 2 * features), bf16),
        jax.ShapeDtypeStruct((rows, half), bf16),
        jax.ShapeDtypeStruct((rows, 2 * half), bf16),
    )
    return pl.pallas_call(
        functools.partial(forward_kernel, experts, len(pieces)),
        out_shape=out_shape,
        in_specs=[pl.BlockSpec(memory_space=pltpu.SMEM)]
        + [pl.BlockSpec(memory_space=pl.ANY)] * len(pieces)
        + [pl.BlockSpec(memory_space=pltpu.VMEM)] * 2,
        out_specs=tuple(pl.BlockSpec(memory_space=pl.ANY) for _ in out_shape),
        scratch_shapes=[
            pltpu.VMEM((rows, features), bf16),
            pltpu.VMEM((rows, features), bf16),
            pltpu.VMEM((rows, LANES), bf16),
            pltpu.VMEM((rows, half), bf16),
            pltpu.VMEM((rows, 2 * half), bf16),
            pltpu.VMEM((rows, features), bf16),
            pltpu.VMEM((2, rows, features // 2), bf16),
            pltpu.SemaphoreType.DMA((len(pieces),)),
            pltpu.SemaphoreType.DMA((len(pieces),)),
            pltpu.SemaphoreType.DMA((len(pieces),)),
            pltpu.SemaphoreType.DMA((8,)),
        ],
        compiler_params=pltpu.CompilerParams(vmem_limit_bytes=VMEM_BYTES),
        cost_estimate=pl.CostEstimate(
            flops=12 * 20 * rows * features * half,
            bytes_accessed=6 * features * half + 8 * rows * features,
            transcendentals=rows * half,
        ),
    )(expert, *pieces, weight_gu, weight_d)


def grads_kernel(n_pieces, n_slots, tile, *refs):
    pieces, refs = refs[:n_pieces], refs[n_pieces:]
    hids, dgus, refs = refs[:n_slots], refs[n_slots : 2 * n_slots], refs[2 * n_slots :]
    gg_ref, gu_ref, gd_ref, x, g, hid, dgu, gg, gu, gd, x_sems, g_sems, a_sems, o_sems = refs
    features, half = gg_ref.shape
    every = pl.ds(0, half)
    first = place_copies(dgus, pl.ds(0, 2 * half), dgu, a_sems.at[0])
    first += place_copies(pieces, pl.ds(0, features), x, x_sems)
    then = place_copies(hids, every, hid, a_sems.at[1])
    then += place_copies(pieces, pl.ds(features, features), g, g_sems)
    for copy in first + then:
        copy.start()
    for copy in first:
        copy.wait()
    sends = []

    def leave(held, place, ref):
        sends.append(
            pltpu.make_async_copy(held.at[place], ref.at[place], o_sems.at[len(sends)])
        )
        sends[-1].start()

    for i in range(features // tile):
        rows = pl.ds(i * tile, tile)
        grad_gu = lax.dot_general(
            x[:, rows], dgu[...], CONTRACT_FIRST, preferred_element_type=jnp.float32
        ).astype(jnp.bfloat16)
        gg[rows] = grad_gu[:, :half]
        gu[rows] = grad_gu[:, half:]
        leave(gg, rows, gg_ref)
        leave(gu, rows, gu_ref)
    for copy in then:
        copy.wait()
    for i in range(half // LANES):
        rows = pl.ds(i * LANES, LANES)
        gd[rows] = lax.dot_general(
            hid[:, rows], g[...], CONTRACT_FIRST, preferred_element_type=jnp.float32
        ).astype(jnp.bfloat16)
        leave(gd, rows, gd_ref)
    for copy in sends:
        copy.wait()


def weight_grads(pieces, hids, dgus):
    features, half = pieces[0].shape[1] // 2 // LANES * LANES, hids[0].shape[1]
    rows = sum(piece.shape[0] for piece in pieces)
    tile = min(256, features)
    bf16 = jnp.bfloat16
    out_shape = (
        jax.ShapeDtypeStruct((features, half), bf16),
        jax.ShapeDtypeStruct((features, half), bf16),
        jax.ShapeDtypeStruct((half, features), bf16),
    )
    return pl.pallas_call(
        functools.partial(grads_kernel, len(pieces), len(hids), tile),
        out_shape=out_shape,
        in_specs=[pl.BlockSpec(memory_space=pl.ANY)] * (len(pieces) + 2 * len(hids)),
        out_specs=tuple(pl.BlockSpec(memory_space=pl.ANY) for _ in out_shape),
        scratch_shapes=[
            pltpu.VMEM((rows, features), bf16),
            pltpu.VMEM((rows, features), bf16),
            pltpu.VMEM((rows, half), bf16),
            pltpu.VMEM((rows, 2 * half), bf16),
            pltpu.VMEM((features, half), bf16),
            pltpu.VMEM((features, half), bf16),
            pltpu.VMEM((half, features), bf16),
            pltpu.SemaphoreType.DMA((len(pieces),)),
            pltpu.SemaphoreType.DMA((len(pieces),)),
            pltpu.SemaphoreType.DMA((2, len(hids))),
            pltpu.SemaphoreType.DMA((2 * (features // tile) + half // LANES,)),
        ],
        compiler_params=pltpu.CompilerParams(vmem_limit_bytes=VMEM_BYTES),
        cost_estimate=pl.CostEstimate(
            flops=1,
            bytes_accessed=6 * features * half + 4 * rows * features,
            transcendentals=0,
        ),
    )(*pieces, *hids, *dgus)


def add(left, right):
    return (left.astype(jnp.float32) + right.astype(jnp.float32)).astype(jnp.bfloat16)


def after(value, *earlier):
    return lax.optimization_barrier((value,) + earlier)[0]


def tick_kernel(in_ref, out_ref):
    pass


def tick(token):
    return pl.pallas_call(
        tick_kernel,
        out_shape=jax.ShapeDtypeStruct(token.shape, token.dtype),
        in_specs=[pl.BlockSpec(memory_space=pl.ANY)],
        out_specs=pl.BlockSpec(memory_space=pl.ANY),
        input_output_aliases={0: 0},
        cost_estimate=pl.CostEstimate(flops=50_000_000_000, bytes_accessed=0, transcendentals=0),
    )(token)


def total_kernel(*refs):
    parts, (mixed_ref, grad_ref) = refs[:-2], refs[-2:]
    features = mixed_ref.shape[1]
    for ref, place in ((mixed_ref, pl.ds(0, features)), (grad_ref, pl.ds(features, features))):
        ref[...] = sum(part[:, place].astype(jnp.float32) for part in parts).astype(jnp.bfloat16)


def total(parts):
    rows, features = parts[0].shape
    shape = jax.ShapeDtypeStruct((rows, features // 2), jnp.bfloat16)
    return pl.pallas_call(
        total_kernel,
        out_shape=(shape, shape),
        compiler_params=pltpu.CompilerParams(vmem_limit_bytes=VMEM_BYTES),
        cost_estimate=pl.CostEstimate(flops=1, bytes_accessed=1, transcendentals=0),
    )(*parts)


def dense_shards(tokens, grad_out, routes, route_weight, w_gate, w_up, w_down):
    n_node, n_local = lax.axis_size("node"), lax.axis_size("local")
    experts = n_node * n_local // 2
    n_z = n_node // 2
    features = tokens.shape[1]
    axes = ("node", "local")
    device = lax.axis_index("node") * n_local + lax.axis_index("local")
    expert = jnp.full((1,), device // 2, jnp.int32)

    def exchange(value, step):
        pairs = [(d, d ^ step((d // n_local) % 2)) for d in range(n_node * n_local)]
        return lax.ppermute(value, axes, pairs)

    first = lambda core: 1 + core
    second = lambda core: 2 - core
    sibling = lambda core: n_local

    def along(z):
        return lambda core: z * 2 * n_local

    rows = tokens.shape[0]
    block = pack(tokens, grad_out, routes, route_weight, experts)
    now = [jnp.zeros((8, LANES), jnp.float32)]

    def start(value, step):
        return exchange(after(value, now[0]), step)

    def wait(value):
        value, now[0] = lax.optimization_barrier((value, now[0]))
        return value

    def turn():
        now[0] = tick(now[0])

    pairs, twos, taken, results, sums = {}, {}, {}, {}, {}

    def spread(z, one, own):
        pairs[z] = wait(jnp.concatenate([own, wait(one)]))
        return start(pairs[z], second), start(pairs[z], sibling)

    def across(z, two):
        twos[z] = wait(two)
        return start(twos[z], sibling)

    def compute(z, pair_there, two_there):
        taken[z] = [pairs[z], twos[z], pair_there, two_there]
        results[z] = forward(expert, [after(t, now[0]) for t in taken[z]], *weights, experts)
        results[z] = [wait(t) for t in results[z]]
        return start(results[z][1], sibling)

    def fold(z, there):
        sums[z] = wait(add(results[z][0], wait(there)))
        return start(sums[z][2 * rows :], second)

    def fold_second(z, there):
        sums[z] = wait(add(sums[z][: 2 * rows], wait(there)))
        return start(sums[z][rows:], first)

    def fold_first(z, there):
        sums[z] = wait(add(sums[z][:rows], wait(there)))
        return start(sums[z], along(z)) if z else sums[z]

    one0 = start(block, first)
    far1 = start(block, along(1))
    far2 = start(block, along(2))
    turn()
    two0, pt0 = spread(0, one0, block)
    weights = stage(after(w_gate, now[0])[0], w_up[0], w_down[0])
    weights = [wait(w) for w in weights]
    turn()
    far1 = wait(far1)
    one1 = start(far1, first)
    far3 = start(block, along(3))
    turn()
    tt0 = across(0, two0)
    two1, pt1 = spread(1, one1, far1)
    turn()
    far2 = wait(far2)
    one2 = start(far2, first)
    back0 = compute(0, pt0, tt0)
    two2, pt2 = spread(2, one2, far2)
    turn()
    far3 = wait(far3)
    one3 = start(far3, first)
    tt1 = across(1, two1)
    turn()
    back1 = compute(1, pt1, tt1)
    two3, pt3 = spread(3, one3, far3)
    tt2 = across(2, two2)
    turn()
    back2 = compute(2, pt2, tt2)
    back1 = fold(1, back1)
    tt3 = across(3, two3)
    turn()
    back2 = fold(2, back2)
    back0 = fold(0, back0)
    back3 = compute(3, pt3, tt3)
    turn()
    back0 = fold_second(0, back0)
    back3 = fold(3, back3)
    back2 = fold_second(2, back2)
    back1 = fold_second(1, back1)
    turn()
    back2 = fold_first(2, back2)
    turn()
    back3 = fold_second(3, back3)
    turn()
    back1 = fold_first(1, back1)
    back0 = fold_first(0, back0)
    turn()
    back3 = fold_first(3, back3)
    order = [0, 1, 2, 3]
    grad_wg, grad_wu, grad_wd = weight_grads(
        [after(piece, now[0]) for z in order for piece in taken[z]],
        [results[z][2] for z in order],
        [results[z][3] for z in order],
    )
    grad_wg = wait(grad_wg)
    arrived = (back0, wait(back2), wait(back1), wait(back3))
    mixed, grad_tokens = total(arrived)
    return (
        mixed,
        grad_tokens,
        grad_wg[None],
        grad_wu[None],
        grad_wd[None],
    )


def solution(mesh):
    n_node, n_local, n_tp = (mesh.shape[name] for name in ("node", "local", "tp"))

    def shards(tokens, grad_out, routes, *rest):
        experts = n_node * n_local // 2
        grid = n_tp == 1 and n_local == 4 and n_node in (4, 8)
        if grid and 2 * routes.shape[1] >= experts:
            return dense_shards(tokens, grad_out, routes, *rest)
        return sparse_shards(tokens, grad_out, routes, *rest)

    return jax.shard_map(
        shards,
        mesh=mesh,
        in_specs=(
            P(("node", "local"), "tp"),
            P(("node", "local"), "tp"),
            P(("node", "local"), None),
            P(("node", "local"), None),
            P(("node", "local"), "tp", None),
            P(("node", "local"), "tp", None),
            P(("node", "local"), None, "tp"),
        ),
        out_specs=(
            P(("node", "local"), "tp"),
            P(("node", "local"), "tp"),
            P(("node", "local"), "tp", None),
            P(("node", "local"), "tp", None),
            P(("node", "local"), None, "tp"),
        ),
        check_vma=False,
    )
```
